128 devices in a mesh: chan: 32 (over x, y_hi, z), win: 4 (over y_lo, core).
Axes of the slice: x: 4, y: 4 (y_hi: 2, y_lo: 2; y = y_hi * 2 + y_lo), z: 4, core: 2. Of those that a mesh axis runs over, the one named last changes fastest.
Arguments:
- records: bfloat16 [256, 1000, 1024], P(('chan', 'win')), may hold values from -50 to 50
Outputs:
- correlations: float32 [1024, 256, 256], P('chan', 'win')
The draws below stay inside these ranges and needn't reach their ends.
All inputs are finite; a program needn't handle non-finite values.
Results may differ from the reference program's by a relative error of at most 0.0023.
Values may be sent and summed in bfloat16 or wider, within the bound.
No kernel may reach another device: no remote copies, remote signals or barrier semaphores. Data moves between devices by JAX's collectives and lax.ppermute only.
A program may use at most 256 MiB of HBM per device.

```python
import math
import jax
import jax.numpy as jnp
from jax import lax

SAMPLES = 1000
BINS = 200
FIRST_BIN = 20
BAND = 256
LAGS = 256
CH_DEV = 32
CHANNELS = 1024
WINDOWS = 256


def draw_records(key, part):
    key = jax.random.fold_in(key, 11)
    key_noise, key_gain, key_window = jax.random.split(key, 3)
    gains = jnp.exp(jax.random.uniform(key_gain, (1, 1, CHANNELS), jnp.float32, math.log(0.2), math.log(5.0)))
    window_scale = jnp.exp(jax.random.uniform(key_window, (WINDOWS, 1, 1), jnp.float32, math.log(0.5), math.log(2.0)))
    noise = jnp.clip(jax.random.normal(key_noise, (WINDOWS, SAMPLES, CHANNELS), jnp.float32), -5.0, 5.0)
    values = noise * gains * window_scale
    return values.astype(jnp.bfloat16)


def setup_inputs(seed: int = 0) -> dict:
    keys = jax.random.split(jax.random.key(seed), 2)
    return {
        "records": draw_records(jax.random.fold_in(keys[1], 71), 0),
    }


def dft_matrix(samples, bin_count):
    times = jnp.arange(samples, dtype=jnp.int32)
    freqs = FIRST_BIN + jnp.arange(bin_count, dtype=jnp.int32)
    turns = times[:, None] * freqs[None, :] % samples
    phase = turns.astype(jnp.float32) * (2.0 * math.pi / samples)
    return jnp.concatenate([jnp.cos(phase), -jnp.sin(phase)], axis=1).astype(jnp.bfloat16)

def lag_matrix(samples, bin_count, lag_count, factor):
    freqs = FIRST_BIN + jnp.arange(bin_count, dtype=jnp.int32)
    shifts = jnp.arange(lag_count, dtype=jnp.int32) - lag_count // 2
    turns = freqs[:, None] * shifts[None, :] % samples
    phase = turns.astype(jnp.float32) * (2.0 * math.pi / samples)
    return jnp.stack([jnp.cos(phase), -jnp.sin(phase)]) * factor

def box_matrix(bin_count):
    places = jnp.arange(bin_count, dtype=jnp.int32)
    near = (jnp.abs(places[:, None] - places[None, :]) <= 4).astype(jnp.float32)
    return near / lax.optimization_barrier(jnp.sum(near, axis=1, keepdims=True))

def whiten(spectra):
    bin_count = spectra.shape[0] // 2
    real_part = spectra[:bin_count]
    imag_part = spectra[bin_count:]
    power = real_part * real_part + imag_part * imag_part
    smooth = jnp.einsum('jk,kwc->jwc', box_matrix(bin_count), jnp.sqrt(power), precision=lax.Precision.HIGHEST)
    level = jnp.sqrt(lax.optimization_barrier(jnp.mean(power, axis=0, keepdims=True)) + 1e-06)
    denom = smooth + 0.25 * level
    return (spectra / jnp.concatenate([denom, denom], axis=0)).astype(jnp.bfloat16)

def skew(part, keep_cols):
    bin_count, row_count, extent = part.shape
    flattened = jnp.pad(part.reshape(bin_count, row_count * extent), ((0, 0), (0, row_count)))
    return flattened.reshape(bin_count, row_count, extent + 1)[:, :, :keep_cols]

def band_stack(left, right, keep_cols):
    bin_count = left.shape[0] // 2
    left = left.astype(jnp.float32)
    right = right.astype(jnp.float32)
    left_rows = jnp.concatenate([left[:bin_count], left[bin_count:]], axis=1)
    first = jnp.concatenate([right[:bin_count], right[bin_count:]], axis=1)
    second = jnp.concatenate([-right[bin_count:], right[:bin_count]], axis=1)
    right_rows = jnp.concatenate([first, second], axis=2)
    products = jnp.einsum('bwc,bwe->bce', left_rows, right_rows, precision=lax.Precision.HIGHEST)
    extent = right.shape[2]
    return jnp.stack([skew(products[:, :, :extent], keep_cols), skew(products[:, :, extent:], keep_cols)], axis=1)

def reference(records):
    dft = dft_matrix(SAMPLES, BINS).astype(jnp.float32)

    def one_window(window):
        spectra = jnp.einsum('sc,sf->fc', window.astype(jnp.float32), dft, precision=lax.Precision.HIGHEST)
        return whiten(spectra[:, None, :])
    whitened = lax.map(one_window, records)
    whitened = jnp.transpose(whitened, (1, 0, 2, 3)).reshape(2 * BINS, WINDOWS, CHANNELS)
    padded = jnp.pad(whitened, ((0, 0), (0, 0), (0, BAND)))
    lag_table = lag_matrix(SAMPLES, BINS, LAGS, 1.0 / (WINDOWS * math.sqrt(BINS)))

    def one_block(block_index):
        begin = block_index * CH_DEV
        left_part = lax.dynamic_slice_in_dim(padded, begin, CH_DEV, 2)
        right_part = lax.dynamic_slice_in_dim(padded, begin, CH_DEV + BAND, 2)
        stacks = band_stack(left_part, right_part, BAND)
        return jnp.einsum('bpco,pbm->com', stacks, lag_table, precision=lax.Precision.HIGHEST)
    blocks = lax.map(one_block, jnp.arange(CHANNELS // CH_DEV, dtype=jnp.int32))
    return blocks.reshape(CHANNELS, BAND, LAGS)
```

```python
import functools
import math

import jax
import jax.numpy as jnp
import ml_dtypes
import numpy as np
from jax import lax
from jax.experimental import pallas as pl
from jax.experimental.pallas import tpu as pltpu
from jax.sharding import PartitionSpec as P

SAMPLES = 1000
BINS = 200
FIRST_BIN = 20
BAND = 256
LAGS = 256
WINDOWS = 256
PER_DEVICE = 2
OWNERS = BINS // PER_DEVICE
OWNER_ROWS = 104
PART_ROWS = PER_DEVICE * OWNER_ROWS
VMEM_LIMIT = 50 * 1024 * 1024


def bins_of_rows():
    rows = np.arange(PART_ROWS)
    owner = rows % OWNER_ROWS
    return np.where(owner < OWNERS, owner * PER_DEVICE + rows // OWNER_ROWS, -1)


def dft_rows():
    bins = bins_of_rows()
    turns = (FIRST_BIN + np.maximum(bins, 0))[:, None] * np.arange(SAMPLES)[None, :] % SAMPLES
    phase = turns * (2.0 * math.pi / SAMPLES)
    both = np.concatenate([np.cos(phase), -np.sin(phase)], axis=0)
    valid = np.concatenate([bins, bins]) >= 0
    return np.where(valid[:, None], both, 0.0).astype(ml_dtypes.bfloat16)


def box_rows():
    bins = bins_of_rows()
    valid = bins >= 0
    near = (np.abs(bins[:, None] - bins[None, :]) <= 4) & valid[:, None] & valid[None, :]
    count = np.maximum(near.sum(axis=1, keepdims=True), 1)
    return near.astype(ml_dtypes.bfloat16), (1.0 / count).astype(np.float32)


def lag_rows():
    freqs = FIRST_BIN + np.arange(BINS)
    shifts = np.arange(LAGS) - LAGS // 2
    phase = (freqs[:, None] * shifts[None, :] % SAMPLES) * (2.0 * math.pi / SAMPLES)
    table = np.stack([np.cos(phase), -np.sin(phase)], axis=1) / (WINDOWS * math.sqrt(BINS))
    table = table.reshape(2 * BINS, LAGS)
    high = table.astype(ml_dtypes.bfloat16)
    low = (table - high.astype(np.float64)).astype(ml_dtypes.bfloat16)
    return np.concatenate([high, low], axis=1)


def dot(left, right, left_dim, right_dim):
    dims = (((left_dim,), (right_dim,)), ((), ()))
    return lax.dot_general(left, right, dims, preferred_element_type=jnp.float32)


def whiten_kernel(records_ref, dft_ref, box_ref, weight_ref, out_ref, rows_ref):
    windows = records_ref.shape[0]
    rows_ref[...] = jnp.zeros_like(rows_ref)
    blocks = rows_ref.shape[0]
    for w in range(windows):
        spectra = dot(dft_ref[...], records_ref[w], 1, 0)
        real_part = spectra[:PART_ROWS]
        imag_part = spectra[PART_ROWS:]
        power = real_part * real_part + imag_part * imag_part
        size = jnp.sqrt(power)
        high = size.astype(jnp.bfloat16)
        low = (size - high.astype(jnp.float32)).astype(jnp.bfloat16)
        smooth = (dot(box_ref[...], high, 1, 0) + dot(box_ref[...], low, 1, 0)) * weight_ref[...]
        level = jnp.sqrt(jnp.sum(power, axis=0, keepdims=True) * (1.0 / BINS) + 1e-06)
        scale = 1.0 / (smooth + 0.25 * level)
        for part, values in enumerate((real_part * scale, imag_part * scale)):
            for b in range(PER_DEVICE):
                piece = values[b * OWNER_ROWS : (b + 1) * OWNER_ROWS]
                place = (part * windows + w) * PER_DEVICE + b
                for n in range(blocks):
                    rows_ref[n, pl.ds(place, OWNER_ROWS, stride=8), :] = piece[:, n * 128 : (n + 1) * 128]
    for n in range(blocks):
        out_ref[:, n * 128 : (n + 1) * 128] = rows_ref[n].astype(jnp.bfloat16)


def whiten(records, devices):
    windows, samples, channels = records.shape
    block = 512
    near, weight = box_rows()
    rows = devices * windows * 2 * PER_DEVICE
    whole = lambda shape: pl.BlockSpec(shape, lambda i: (0, 0))
    return pl.pallas_call(
        whiten_kernel,
        grid=(channels // block,),
        in_specs=[
            pl.BlockSpec((windows, samples, block), lambda i: (0, 0, i)),
            whole((2 * PART_ROWS, samples)),
            whole((PART_ROWS, PART_ROWS)),
            whole((PART_ROWS, 1)),
        ],
        out_specs=pl.BlockSpec((rows, block), lambda i: (0, i)),
        out_shape=jax.ShapeDtypeStruct((rows, channels), jnp.bfloat16),
        scratch_shapes=[pltpu.VMEM((block // 128, rows, 128), jnp.float32)],
        compiler_params=pltpu.CompilerParams(vmem_limit_bytes=VMEM_LIMIT),
        name="whiten",
    )(records, jnp.asarray(dft_rows()), jnp.asarray(near), jnp.asarray(weight))


def stack_kernel(rows_ref, flip_ref, out_ref):
    row_count, channels = rows_ref.shape
    block = flip_ref.shape[0]
    row = lax.broadcasted_iota(jnp.int32, (1, 8, block), 1)
    sign = jnp.where(row < 4, 1.0, -1.0)
    column = lax.broadcasted_iota(jnp.int32, (1, row_count), 1)
    lane = lax.broadcasted_iota(jnp.int32, (8, 16, 128), 2)
    for c in range(channels // block):
        begin = c * block
        extent = min(2 * block, channels - begin)
        plain = rows_ref[:, begin : begin + block]
        turned = plain.astype(jnp.float32).reshape(row_count // 8, 8, block)
        turned = (pltpu.roll(turned, 4, 1) * sign).reshape(row_count, block).astype(jnp.bfloat16)
        flipped = [dot(flip_ref[...], side, 1, 1) for side in (plain, turned)]
        sides = []
        for b in range(PER_DEVICE):
            keep = jnp.where(column % PER_DEVICE == b, 1.0, 0.0)
            sides += [(side * keep).astype(jnp.bfloat16) for side in flipped]
        left = jnp.concatenate(sides, axis=0)
        products = dot(left, rows_ref[:, begin : begin + extent], 1, 0)
        for p in range(2 * PER_DEVICE):
            product = products[p * block : (p + 1) * block]
            if extent < 2 * block:
                product = jnp.concatenate([product, jnp.zeros_like(product)], axis=1)
            skewed = pltpu.roll(product, block + 1, 1, stride=1, stride_axis=0)[:, :BAND]
            halves = skewed.reshape(8, 2, 16, BAND)
            for q in range(BAND // 128):
                first = halves[:, 1, :, q * 128 : (q + 1) * 128]
                second = halves[:, 0, :, q * 128 : (q + 1) * 128]
                even = jnp.where(lane < 64, first, pltpu.roll(second, 64, 2)).astype(jnp.bfloat16)
                odd = jnp.where(lane < 64, pltpu.roll(first, 64, 2), second).astype(jnp.bfloat16)
                for i in range(8):
                    out_ref[c * 8 + 7 - i, 2 * q, p * 16 : (p + 1) * 16, :] = even[i]
                    out_ref[c * 8 + 7 - i, 2 * q + 1, p * 16 : (p + 1) * 16, :] = odd[i]


def stack(rows, chan_size, win_size):
    return pl.pallas_call(
        stack_kernel,
        out_shape=jax.ShapeDtypeStruct((chan_size, win_size, 64, 128), jnp.bfloat16),
        in_specs=[pl.BlockSpec(memory_space=pltpu.VMEM)] * 2,
        out_specs=pl.BlockSpec(memory_space=pltpu.VMEM),
        compiler_params=pltpu.CompilerParams(vmem_limit_bytes=VMEM_LIMIT),
        name="stack",
    )(rows, jnp.asarray(np.eye(256)[::-1], jnp.bfloat16))


def lag_kernel(stacks_ref, table_ref, out_ref, wide_ref):
    step = pl.program_id(0)

    @pl.when(step == 0)
    def _():
        wide_ref[...] = stacks_ref[...].astype(jnp.float32)

    left = wide_ref[pl.ds(15 - step, 2 * BINS, stride=16), :].astype(jnp.bfloat16)
    both = dot(left, table_ref[...], 0, 0)
    lags = both[:, :LAGS] + both[:, LAGS:]
    out_ref[...] = lags.reshape(2, 1, 64, LAGS)


def lag_transform(stacks):
    used = 2 * BINS * 16
    out = pl.pallas_call(
        lag_kernel,
        grid=(16,),
        in_specs=[
            pl.BlockSpec((used, 128), lambda i: (0, 0)),
            pl.BlockSpec((2 * BINS, 2 * LAGS), lambda i: (0, 0)),
        ],
        out_specs=pl.BlockSpec((2, 1, 64, LAGS), lambda i: (0, i, 0, 0)),
        out_shape=jax.ShapeDtypeStruct((2, 16, 64, LAGS), jnp.float32),
        scratch_shapes=[pltpu.VMEM((used, 128), jnp.float32)],
        compiler_params=pltpu.CompilerParams(vmem_limit_bytes=VMEM_LIMIT),
        name="lag_transform",
    )(stacks, jnp.asarray(lag_rows()))
    return out.reshape(32, 64, LAGS)


def per_device(chan_size, win_size, records):
    devices = chan_size * win_size
    axes = ("chan", "win")
    channels = records.shape[2]
    rows = whiten(records, devices).reshape(devices, 8, channels)
    rows = lax.all_to_all(rows, axes, split_axis=0, concat_axis=0, tiled=True)
    stacks = stack(rows.reshape(devices * 8, channels), chan_size, win_size)
    stacks = stacks.reshape(devices, 64, 128)
    stacks = lax.all_to_all(stacks, axes, split_axis=0, concat_axis=0, tiled=True)
    return lag_transform(stacks.reshape(devices * 64, 128))


def solution(mesh):
    in_specs = (P(("chan", "win"), None, None),)
    out_specs = P("chan", "win", None)
    body = functools.partial(per_device, mesh.shape["chan"], mesh.shape["win"])
    return jax.shard_map(body, mesh=mesh, in_specs=in_specs, out_specs=out_specs, check_vma=False)
```

```python
import functools
import math

import jax
import jax.numpy as jnp
import ml_dtypes
import numpy as np
from jax import lax
from jax.experimental import pallas as pl
from jax.experimental.pallas import tpu as pltpu
from jax.sharding import PartitionSpec as P

SAMPLES = 1000
BINS = 200
FIRST_BIN = 20
BAND = 256
LAGS = 256
WINDOWS = 256
OWNERS = BINS // 2
OWNER_ROWS = 104
ROWS = 2 * OWNER_ROWS
VMEM_LIMIT = 50 * 1024 * 1024


def dft_rows():
    turns = (FIRST_BIN + np.arange(BINS))[:, None] * np.arange(SAMPLES)[None, :] % SAMPLES
    phase = turns * (2.0 * math.pi / SAMPLES)
    table = np.stack([np.cos(phase), -np.sin(phase)]).reshape(4, OWNERS, SAMPLES)
    table = np.pad(table, ((0, 0), (0, OWNER_ROWS - OWNERS), (0, 0)))
    return table.reshape(4 * OWNER_ROWS, SAMPLES).astype(ml_dtypes.bfloat16)


def lag_rows():
    shifts = np.arange(LAGS) - LAGS // 2
    bins = np.arange(BINS).reshape(2, OWNERS).T.reshape(-1)
    phase = ((FIRST_BIN + bins)[:, None] * shifts[None, :] % SAMPLES) * (2.0 * math.pi / SAMPLES)
    table = np.stack([np.cos(phase), -np.sin(phase)], axis=1) / (WINDOWS * math.sqrt(BINS))
    table = table.reshape(2 * BINS, LAGS)
    high = table.astype(ml_dtypes.bfloat16)
    low = (table - high.astype(np.float64)).astype(ml_dtypes.bfloat16)
    return np.concatenate([high, low], axis=1)


def dot(left, right, left_dim, right_dim):
    dims = (((left_dim,), (right_dim,)), ((), ()))
    return lax.dot_general(left, right, dims, preferred_element_type=jnp.float32)


def params():
    return pltpu.CompilerParams(vmem_limit_bytes=VMEM_LIMIT)


def cost(flops, bytes_accessed):
    return pl.CostEstimate(flops=flops, bytes_accessed=bytes_accessed, transcendentals=0)


def bin_of(row):
    return jnp.where(row < OWNER_ROWS, row, row - (OWNER_ROWS - OWNERS))


def near_matrix():
    row = lax.broadcasted_iota(jnp.int32, (ROWS, ROWS), 0)
    column = lax.broadcasted_iota(jnp.int32, (ROWS, ROWS), 1)
    near = jnp.abs(bin_of(row) - bin_of(column)) <= 4
    near = near & (row % OWNER_ROWS < OWNERS) & (column % OWNER_ROWS < OWNERS)
    return jnp.where(near, 1.0, 0.0).astype(jnp.bfloat16)


def whiten_kernel(records_ref, dft_ref, out_ref, rows_ref):
    windows = records_ref.shape[0]
    blocks, row_count, _ = rows_ref.shape
    near = near_matrix()
    place = bin_of(lax.broadcasted_iota(jnp.int32, (ROWS, 1), 0))
    count = jnp.minimum(place + 4, BINS - 1) - jnp.maximum(place - 4, 0) + 1
    weight = 1.0 / count.astype(jnp.float32)

    @pl.when(pl.program_id(0) == 0)
    def _():
        rest = row_count - OWNER_ROWS * 8
        rows_ref[:, OWNER_ROWS * 8 :, :] = jnp.zeros((blocks, rest, 128), jnp.float32)

    for w in range(windows):
        spectra = dot(dft_ref[...], records_ref[w], 1, 0)
        real_part = spectra[:ROWS]
        imag_part = spectra[ROWS:]
        power = real_part * real_part + imag_part * imag_part
        size = jnp.sqrt(power)
        high = size.astype(jnp.bfloat16)
        low = (size - high.astype(jnp.float32)).astype(jnp.bfloat16)
        smooth = (dot(near, high, 1, 0) + dot(near, low, 1, 0)) * weight
        level = jnp.sqrt(jnp.sum(power, axis=0, keepdims=True) * (1.0 / BINS) + 1e-06)
        scale = 1.0 / (smooth + 0.25 * level)
        for part, values in enumerate((real_part * scale, imag_part * scale)):
            place = part * windows + w
            for n in range(blocks):
                piece = values[:, n * 128 : (n + 1) * 128]
                for b in range(2):
                    rows_ref[n, pl.ds(b * 4 + place, OWNER_ROWS, stride=8), :] = piece[
                        b * OWNER_ROWS : (b + 1) * OWNER_ROWS
                    ]
    for n in range(blocks):
        out_ref[:, n * 128 : (n + 1) * 128] = rows_ref[n].astype(jnp.bfloat16)


def whiten(records, devices):
    windows, samples, channels = records.shape
    rows = devices * 8
    block = 512
    return pl.pallas_call(
        whiten_kernel,
        grid=(channels // block,),
        in_specs=[
            pl.BlockSpec((windows, samples, block), lambda i: (0, 0, i)),
            pl.BlockSpec((2 * ROWS, samples), lambda i: (0, 0)),
        ],
        out_specs=pl.BlockSpec((rows, block), lambda i: (0, i)),
        out_shape=jax.ShapeDtypeStruct((rows, channels), jnp.bfloat16),
        scratch_shapes=[pltpu.VMEM((block // 128, rows, 128), jnp.float32)],
        compiler_params=params(),
        cost_estimate=cost(2 * windows * samples * channels * 2 * BINS, records.size * 2 + rows * channels * 2),
        name="whiten",
    )(records, jnp.asarray(dft_rows()))


def stack_kernel(rows_ref, out_ref, plain_ref, turned_ref):
    row_count, channels = rows_ref.shape
    block = 256
    row = lax.broadcasted_iota(jnp.int32, (1, 8, block), 1)
    for begin in range(0, channels, block):
        wide = rows_ref[:, begin : begin + block].astype(jnp.float32).reshape(row_count // 16, 2, 8, block)
        even, odd = wide[:, 0], wide[:, 1]
        halves = (
            jnp.where(row < 4, even, pltpu.roll(odd, 4, 1)),
            jnp.where(row < 4, pltpu.roll(even, 4, 1), odd),
        )
        for b, half in enumerate(halves):
            turned = jnp.where(row // 2 % 2 == 0, pltpu.roll(half, 6, 1), -pltpu.roll(half, 2, 1))
            for ref, value in ((plain_ref, half), (turned_ref, turned)):
                ref[b, :, begin : begin + block] = value.reshape(row_count // 2, block).astype(jnp.bfloat16)
    row = lax.broadcasted_iota(jnp.int32, (block, block), 0)
    column = lax.broadcasted_iota(jnp.int32, (block, block), 1)
    flip = jnp.where(row + column == block - 1, 1.0, 0.0).astype(jnp.bfloat16)
    lane = lax.broadcasted_iota(jnp.int32, (16, 128), 1)
    for b in range(2):
        for c in range(channels // block):
            begin = c * block
            sides = [dot(flip, ref[b, :, begin : begin + block], 1, 1) for ref in (plain_ref, turned_ref)]
            sides = [side.astype(jnp.bfloat16) for side in sides]
            for u in range(2):
                left = jnp.concatenate([side[u * 128 : (u + 1) * 128] for side in sides], axis=0)
                right = begin + 128 * (1 - u)
                extent = min(384, channels - right)
                products = dot(left, plain_ref[b, :, right : right + extent], 1, 0)
                if extent < 384:
                    products = jnp.concatenate([products, jnp.zeros((256, 384 - extent), jnp.float32)], axis=1)
                for p in range(2):
                    item = (b * 2 + p) * 16
                    for i in range(4):
                        r = p * 128 + i * 32
                        second = pltpu.roll(products[r : r + 16], (321 + 32 * i) % 384, 1, stride=1, stride_axis=0)
                        first = pltpu.roll(products[r + 16 : r + 32], (273 + 32 * i) % 384, 1, stride=1, stride_axis=0)
                        where = c * 8 + 7 - u * 4 - i
                        for q in range(2):
                            now = slice(q * 128, (q + 1) * 128)
                            then = slice((q + 1) * 128, (q + 2) * 128)
                            low = jnp.where(lane < 64, first[:, now], second[:, now])
                            high = jnp.where(lane < 64, second[:, then], first[:, now])
                            out_ref[where, 2 * q, item : item + 16, :] = low.astype(jnp.bfloat16)
                            out_ref[where, 2 * q + 1, item : item + 16, :] = high.astype(jnp.bfloat16)


def stack(rows, chan_size, win_size):
    row_count, channels = rows.shape
    return pl.pallas_call(
        stack_kernel,
        out_shape=jax.ShapeDtypeStruct((chan_size, win_size, 64, 128), jnp.bfloat16),
        in_specs=[pl.BlockSpec(memory_space=pltpu.VMEM)],
        out_specs=pl.BlockSpec(memory_space=pltpu.VMEM),
        scratch_shapes=[pltpu.VMEM((2, row_count // 2, channels), jnp.bfloat16)] * 2,
        compiler_params=params(),
        cost_estimate=cost(4 * 2 * 1024 * 512 * 512, 4 * 1024 * 1024),
        name="stack",
    )(rows)


def lag_kernel(steps, swap_ref, table_ref, stacks_ref, out_ref, wide_ref):
    step = pl.program_id(0)
    items = table_ref.shape[0]
    each = 16 // steps

    @pl.when(step == 0)
    def _():
        wide_ref[...] = stacks_ref[...].astype(jnp.float32)

    sides = []
    for n in range(each):
        place = 15 - (step * each + n)
        sides.append(wide_ref[pl.ds(place, items, stride=16), :].astype(jnp.bfloat16))
    both = dot(jnp.concatenate(sides, axis=1), table_ref[...], 0, 0)
    lags = both[:, :LAGS] + both[:, LAGS:]
    swap = swap_ref[0]
    for n in range(each):
        for h in range(2):
            r = n * 128 + h * 64
            out_ref[(h + swap) % 2, n] = lags[r : r + 64]


def lag_transform(stacks, swap):
    steps = 4
    table = jnp.asarray(lag_rows())
    rows = 2 * BINS * 16
    out = pl.pallas_call(
        functools.partial(lag_kernel, steps),
        grid=(steps,),
        in_specs=[
            pl.BlockSpec(memory_space=pltpu.SMEM),
            pl.BlockSpec(table.shape, lambda i: (0, 0)),
            pl.BlockSpec((rows, 128), lambda i: (0, 0)),
        ],
        out_specs=pl.BlockSpec((2, 16 // steps, 64, LAGS), lambda i: (0, i, 0, 0)),
        out_shape=jax.ShapeDtypeStruct((2, 16, 64, LAGS), jnp.float32),
        scratch_shapes=[pltpu.VMEM((rows, 128), jnp.float32)],
        compiler_params=params(),
        cost_estimate=cost(4 * 2 * BINS * 2048 * 256, 4 * 1024 * 1024),
        name="lag_transform",
    )(swap, table, stacks)
    return out.reshape(32, 64, LAGS)


def per_device(chan_size, win_size, records):
    devices = chan_size * win_size
    axes = ("chan", "win")
    channels = records.shape[2]
    rows = whiten(records, devices).reshape(devices, 8, channels)
    rows = lax.all_to_all(rows, axes, split_axis=0, concat_axis=0, tiled=True)
    stacks = stack(rows.reshape(devices * 8, channels), chan_size, win_size)
    stacks = stacks.reshape(devices, 64, 128)
    stacks = lax.all_to_all(stacks, axes, split_axis=0, concat_axis=0, tiled=True)
    swap = jnp.full((1,), lax.axis_index("win") % 2, jnp.int32)
    return lag_transform(stacks.reshape(devices * 64, 128), swap)


def solution(mesh):
    in_specs = (P(("chan", "win"), None, None),)
    out_specs = P("chan", "win", None)
    body = functools.partial(per_device, mesh.shape["chan"], mesh.shape["win"])
    return jax.shard_map(body, mesh=mesh, in_specs=in_specs, out_specs=out_specs, check_vma=False)
```

```python
import functools
import math

import jax
import jax.numpy as jnp
import ml_dtypes
import numpy as np
from jax import lax
from jax.experimental import pallas as pl
from jax.experimental.pallas import tpu as pltpu
from jax.sharding import PartitionSpec as P

SAMPLES = 1000
BINS = 200
FIRST_BIN = 20
BAND = 256
LAGS = 256
WINDOWS = 256
OWNERS = BINS // 2
OWNER_ROWS = 104
ROWS = 2 * OWNER_ROWS


def cos_sin(freqs, times):
    turns = freqs * times
    turns = turns - SAMPLES * jnp.floor(turns * (1.0 / SAMPLES) + 0.5)
    phase = turns * (2.0 * math.pi / SAMPLES)
    return jnp.cos(phase), jnp.sin(phase)


def dft_rows():
    def ramp(rows, axis):
        return lax.broadcasted_iota(jnp.int32, (rows, SAMPLES), axis).astype(jnp.float32)

    near_cos, near_sin = cos_sin(ramp(8, 0), ramp(8, 1))
    steps = OWNER_ROWS // 8
    place = ramp(2 * 16, 0)
    base = FIRST_BIN + 8.0 * place + jnp.where(place < 16, 0.0, OWNERS - 8.0 * 16)
    base_cos, base_sin = cos_sin(base, ramp(2 * 16, 1))
    real_rows, imag_rows = [], []
    for b in range(2):
        for n in range(steps):
            row = b * 16 + n
            far_cos, far_sin = base_cos[row : row + 1], base_sin[row : row + 1]
            real_rows.append(far_cos * near_cos - far_sin * near_sin)
            imag_rows.append(-far_sin * near_cos - far_cos * near_sin)
    table = jnp.concatenate(real_rows + imag_rows, axis=0)
    place = lax.broadcasted_iota(jnp.int32, (2 * ROWS, 1), 0) % OWNER_ROWS
    return jnp.where(place < OWNERS, table, 0.0).astype(jnp.bfloat16)


def lag_rows():
    shifts = np.arange(LAGS) - LAGS // 2
    bins = np.arange(BINS).reshape(2, OWNERS).T.reshape(-1)
    phase = ((FIRST_BIN + bins)[:, None] * shifts[None, :] % SAMPLES) * (2.0 * math.pi / SAMPLES)
    table = np.stack([np.cos(phase), -np.sin(phase)], axis=1) / (WINDOWS * math.sqrt(BINS))
    table = table.reshape(2 * BINS, LAGS)
    high = table.astype(ml_dtypes.bfloat16)
    low = (table - high.astype(np.float64)).astype(ml_dtypes.bfloat16)
    return np.concatenate([high, low], axis=1)


def dot(left, right, left_dim, right_dim):
    dims = (((left_dim,), (right_dim,)), ((), ()))
    return lax.dot_general(left, right, dims, preferred_element_type=jnp.float32)


def params(mebibytes):
    return pltpu.CompilerParams(vmem_limit_bytes=mebibytes * 1024 * 1024)


def cost(flops, bytes_accessed):
    return pl.CostEstimate(flops=flops, bytes_accessed=bytes_accessed, transcendentals=0)


def bin_of(row):
    return jnp.where(row < OWNER_ROWS, row, row - (OWNER_ROWS - OWNERS))


def near_matrix():
    row = lax.broadcasted_iota(jnp.int32, (ROWS, ROWS), 0)
    column = lax.broadcasted_iota(jnp.int32, (ROWS, ROWS), 1)
    near = jnp.abs(bin_of(row) - bin_of(column)) <= 4
    near = near & (row % OWNER_ROWS < OWNERS) & (column % OWNER_ROWS < OWNERS)
    return jnp.where(near, 1.0, 0.0).astype(jnp.bfloat16)


def whiten_kernel(chunk, records_hbm, out_ref, records_ref, dft_ref, rows_ref, sems):
    windows, _, channels = records_ref.shape
    row_count = rows_ref.shape[1]
    pieces = [(0, begin, chunk) for begin in range(0, channels, chunk)]
    pieces += [(w, 0, channels) for w in range(1, windows)]
    copies = []
    for n, (w, begin, extent) in enumerate(pieces):
        where = (w, slice(None), pl.ds(begin, extent))
        copies.append(pltpu.make_async_copy(records_hbm.at[where], records_ref.at[where], sems.at[n]))
        copies[-1].start()
    near = near_matrix()
    twice = jnp.concatenate([near, near], axis=1)
    place = bin_of(lax.broadcasted_iota(jnp.int32, (ROWS, 1), 0))
    count = jnp.minimum(place + 4, BINS - 1) - jnp.maximum(place - 4, 0) + 1
    weight = 1.0 / count.astype(jnp.float32)
    rest = row_count - OWNER_ROWS * 8
    out_ref[OWNER_ROWS * 8 :, :] = jnp.zeros((rest, channels), jnp.bfloat16)
    dft_ref[...] = dft_rows()
    for copy, (w, begin, extent) in zip(copies, pieces):
        copy.wait()
        spectra = dot(dft_ref[...], records_ref[w, :, begin : begin + extent], 1, 0)
        real_part = spectra[:ROWS]
        imag_part = spectra[ROWS:]
        power = real_part * real_part + imag_part * imag_part
        size = jnp.sqrt(power)
        high = size.astype(jnp.bfloat16)
        low = (size - high.astype(jnp.float32)).astype(jnp.bfloat16)
        smooth = dot(twice, jnp.concatenate([high, low], axis=0), 1, 0) * weight
        level = jnp.sqrt(jnp.sum(power, axis=0, keepdims=True) * (1.0 / BINS) + 1e-06)
        scale = 1.0 / (smooth + 0.25 * level)
        for part, values in enumerate((real_part * scale, imag_part * scale)):
            place = part * windows + w
            for n in range(extent // 128):
                piece = values[:, n * 128 : (n + 1) * 128]
                for b in range(2):
                    rows_ref[begin // 128 + n, pl.ds(b * 4 + place, OWNER_ROWS, stride=8), :] = piece[
                        b * OWNER_ROWS : (b + 1) * OWNER_ROWS
                    ]
        if w == windows - 1:
            for n in range(channels // 128):
                kept = rows_ref[n, : OWNER_ROWS * 8].astype(jnp.bfloat16)
                out_ref[: OWNER_ROWS * 8, n * 128 : (n + 1) * 128] = kept


def whiten(records, devices):
    windows, samples, channels = records.shape
    rows = devices * 8
    chunk = 1024
    return pl.pallas_call(
        functools.partial(whiten_kernel, chunk),
        in_specs=[pl.BlockSpec(memory_space=pltpu.HBM)],
        out_specs=pl.BlockSpec(memory_space=pltpu.VMEM),
        out_shape=jax.ShapeDtypeStruct((rows, channels), jnp.bfloat16),
        scratch_shapes=[
            pltpu.VMEM(records.shape, jnp.bfloat16),
            pltpu.VMEM((2 * ROWS, samples), jnp.bfloat16),
            pltpu.VMEM((channels // 128, rows, 128), jnp.float32),
            pltpu.SemaphoreType.DMA((windows - 1 + channels // chunk,)),
        ],
        compiler_params=params(50),
        cost_estimate=cost(2 * windows * samples * channels * 2 * BINS, records.size * 2 + rows * channels * 2),
        name="whiten",
    )(records)


def stack_kernel(rows_ref, out_ref, plain_ref, turned_ref):
    row_count, channels = rows_ref.shape
    block = 256
    row = lax.broadcasted_iota(jnp.int32, (1, 8, block), 1)
    for begin in range(0, channels, block):
        wide = rows_ref[:, begin : begin + block].astype(jnp.float32).reshape(row_count // 16, 2, 8, block)
        even, odd = wide[:, 0], wide[:, 1]
        halves = (
            jnp.where(row < 4, even, pltpu.roll(odd, 4, 1)),
            jnp.where(row < 4, pltpu.roll(even, 4, 1), odd),
        )
        for b, half in enumerate(halves):
            turned = jnp.where(row // 2 % 2 == 0, pltpu.roll(half, 6, 1), -pltpu.roll(half, 2, 1))
            for ref, value in ((plain_ref, half), (turned_ref, turned)):
                ref[b, :, begin : begin + block] = value.reshape(row_count // 2, block).astype(jnp.bfloat16)
    row = lax.broadcasted_iota(jnp.int32, (block, block), 0)
    column = lax.broadcasted_iota(jnp.int32, (block, block), 1)
    flip = jnp.where(row + column == block - 1, 1.0, 0.0).astype(jnp.bfloat16)
    lane = lax.broadcasted_iota(jnp.int32, (16, 128), 1)
    for c in range(channels // block):
        begin = c * block
        sources = [ref[b, :, begin : begin + block] for b in range(2) for ref in (plain_ref, turned_ref)]
        flipped = dot(flip, jnp.concatenate(sources, axis=0), 1, 1).astype(jnp.bfloat16)
        count = row_count // 2
        for b in range(2):
            sides = [flipped[:, (2 * b + n) * count : (2 * b + n + 1) * count] for n in range(2)]
            left = jnp.concatenate(sides, axis=0)
            extent = min(512, channels - begin)
            products = dot(left, plain_ref[b, :, begin : begin + extent], 1, 0)
            if extent < 512:
                products = jnp.concatenate([products, jnp.zeros((512, 512 - extent), jnp.float32)], axis=1)
            for p in range(2):
                item = (b * 2 + p) * 16
                for i in range(8):
                    u, j = i // 4, i % 4
                    r = p * 256 + i * 32
                    part = products[r : r + 32, 128 * (1 - u) : 128 * (1 - u) + 384]
                    second = pltpu.roll(part[:16], (321 + 32 * j) % 384, 1, stride=1, stride_axis=0)
                    first = pltpu.roll(part[16:], (273 + 32 * j) % 384, 1, stride=1, stride_axis=0)
                    where = c * 8 + 7 - i
                    for q in range(2):
                        now = slice(q * 128, (q + 1) * 128)
                        then = slice((q + 1) * 128, (q + 2) * 128)
                        low = jnp.where(lane < 64, first[:, now], second[:, now])
                        high = jnp.where(lane < 64, second[:, then], first[:, now])
                        out_ref[where, 2 * q, item : item + 16, :] = low.astype(jnp.bfloat16)
                        out_ref[where, 2 * q + 1, item : item + 16, :] = high.astype(jnp.bfloat16)


def stack(rows, chan_size, win_size):
    row_count, channels = rows.shape
    return pl.pallas_call(
        stack_kernel,
        out_shape=jax.ShapeDtypeStruct((chan_size, win_size, 64, 128), jnp.bfloat16),
        in_specs=[pl.BlockSpec(memory_space=pltpu.VMEM)],
        out_specs=pl.BlockSpec(memory_space=pltpu.VMEM),
        scratch_shapes=[pltpu.VMEM((2, row_count // 2, channels), jnp.bfloat16)] * 2,
        compiler_params=params(24),
        cost_estimate=cost(4 * 2 * 1024 * 512 * 512, 4 * 1024 * 1024),
        name="stack",
    )(rows)


def lag_kernel(parts, swap_ref, table_ref, stacks_ref, out_hbm, wide_ref, out_ref, sems):
    items = table_ref.shape[0]
    each = 16 // parts
    wide_ref[...] = stacks_ref[...].astype(jnp.float32)
    swap = swap_ref[0]
    copies = []
    for part in range(parts):
        sides = []
        for n in range(each):
            place = 15 - (part * each + n)
            sides.append(wide_ref[pl.ds(place, items, stride=16), :].astype(jnp.bfloat16))
        both = dot(jnp.concatenate(sides, axis=1), table_ref[...], 0, 0)
        lags = both[:, :LAGS] + both[:, LAGS:]
        for n in range(each):
            for h in range(2):
                r = n * 128 + h * 64
                out_ref[(h + swap) % 2, part * each + n] = lags[r : r + 64]
        where = (slice(None), pl.ds(part * each, each))
        copies.append(pltpu.make_async_copy(out_ref.at[where], out_hbm.at[where], sems.at[part]))
        copies[-1].start()
    for copy in copies:
        copy.wait()


def lag_transform(stacks, swap):
    parts = 4
    table = jnp.asarray(lag_rows())
    rows = 2 * BINS * 16
    shape = (2, 16, 64, LAGS)
    out = pl.pallas_call(
        functools.partial(lag_kernel, parts),
        grid=(1,),
        in_specs=[
            pl.BlockSpec(memory_space=pltpu.SMEM),
            pl.BlockSpec(table.shape, lambda i: (0, 0)),
            pl.BlockSpec((rows, 128), lambda i: (0, 0)),
        ],
        out_specs=pl.BlockSpec(memory_space=pltpu.HBM),
        out_shape=jax.ShapeDtypeStruct(shape, jnp.float32),
        scratch_shapes=[
            pltpu.VMEM((rows, 128), jnp.float32),
            pltpu.VMEM(shape, jnp.float32),
            pltpu.SemaphoreType.DMA((parts,)),
        ],
        compiler_params=params(24),
        cost_estimate=cost(4 * 2 * BINS * 2048 * 256, 4 * 1024 * 1024),
        name="lag_transform",
    )(swap, table, stacks)
    return out.reshape(32, 64, LAGS)


def per_device(chan_size, win_size, records):
    devices = chan_size * win_size
    axes = ("chan", "win")
    channels = records.shape[2]
    swap = jnp.full((1,), lax.axis_index("win") % 2, jnp.int32)
    rows = whiten(records, devices).reshape(devices, 8, channels)
    rows, swap = lax.optimization_barrier((rows, swap))
    rows = lax.all_to_all(rows, axes, split_axis=0, concat_axis=0, tiled=True)
    stacks = stack(rows.reshape(devices * 8, channels), chan_size, win_size)
    stacks = stacks.reshape(devices, 64, 128)
    stacks = lax.all_to_all(stacks, axes, split_axis=0, concat_axis=0, tiled=True)
    return lag_transform(stacks.reshape(devices * 64, 128), swap)


def solution(mesh):
    in_specs = (P(("chan", "win"), None, None),)
    out_specs = P("chan", "win", None)
    body = functools.partial(per_device, mesh.shape["chan"], mesh.shape["win"])
    return jax.shard_map(body, mesh=mesh, in_specs=in_specs, out_specs=out_specs, check_vma=False)
```

```python
import functools
import math

import jax
import jax.numpy as jnp
import ml_dtypes
import numpy as np
from jax import lax
from jax.experimental import pallas as pl
from jax.experimental.pallas import tpu as pltpu
from jax.sharding import PartitionSpec as P

SAMPLES = 1000
BINS = 200
FIRST_BIN = 20
BAND = 256
LAGS = 256
WINDOWS = 256
GROUP = 8
REACH = 384


def cos_sin(freqs, times):
    turns = freqs * times
    turns = turns - SAMPLES * jnp.floor(turns * (1.0 / SAMPLES) + 0.5)
    phase = turns * (2.0 * math.pi / SAMPLES)
    return jnp.cos(phase), jnp.sin(phase)


def dft_rows():
    def ramp(rows, axis):
        return lax.broadcasted_iota(jnp.int32, (rows, SAMPLES), axis).astype(jnp.float32)

    near_cos, near_sin = cos_sin(ramp(8, 0), ramp(8, 1))
    base_cos, base_sin = cos_sin(FIRST_BIN + 8.0 * ramp(32, 0), ramp(32, 1))
    real_rows, imag_rows = [], []
    for n in range(BINS // 8):
        far_cos, far_sin = base_cos[n : n + 1], base_sin[n : n + 1]
        real_rows.append(far_cos * near_cos - far_sin * near_sin)
        imag_rows.append(-far_sin * near_cos - far_cos * near_sin)
    return jnp.concatenate(real_rows + imag_rows, axis=0).astype(jnp.bfloat16)


def lag_rows(devices):
    owner = np.arange(devices)
    third = devices + owner // 2
    bins = np.stack([owner, owner, third], axis=1).reshape(-1)
    part = np.stack([0 * owner, 0 * owner + 1, owner % 2], axis=1).reshape(-1)
    last = np.arange(BINS - GROUP, BINS)
    bins = np.concatenate([bins, np.repeat(last, 2)])
    part = np.concatenate([part, np.tile([0, 1], GROUP)])
    shifts = np.arange(LAGS) - LAGS // 2
    phase = ((FIRST_BIN + bins)[:, None] * shifts[None, :] % SAMPLES) * (2.0 * math.pi / SAMPLES)
    table = np.where(part[:, None] == 0, np.cos(phase), -np.sin(phase)) / (WINDOWS * math.sqrt(BINS))
    high = table.astype(ml_dtypes.bfloat16)
    low = (table - high.astype(np.float64)).astype(ml_dtypes.bfloat16)
    return np.concatenate([high, low], axis=1)


def dot(left, right, left_dim, right_dim):
    dims = (((left_dim,), (right_dim,)), ((), ()))
    return lax.dot_general(left, right, dims, preferred_element_type=jnp.float32)


def params(mebibytes):
    return pltpu.CompilerParams(vmem_limit_bytes=mebibytes * 1024 * 1024)


def cost(flops, bytes_accessed):
    return pl.CostEstimate(flops=flops, bytes_accessed=bytes_accessed, transcendentals=0)


def whiten_kernel(devices, records_hbm, out_ref, records_ref, dft_ref, rows_ref, sems):
    windows, _, channels = records_ref.shape
    copies = []
    for w in range(windows):
        copies.append(pltpu.make_async_copy(records_hbm.at[w], records_ref.at[w], sems.at[w]))
        copies[-1].start()
    row = lax.broadcasted_iota(jnp.int32, (BINS, BINS), 0)
    column = lax.broadcasted_iota(jnp.int32, (BINS, BINS), 1)
    near = jnp.where(jnp.abs(row - column) <= 4, 1.0, 0.0).astype(jnp.bfloat16)
    place = lax.broadcasted_iota(jnp.int32, (BINS, 1), 0)
    count = jnp.minimum(place + 4, BINS - 1) - jnp.maximum(place - 4, 0) + 1
    weight = 1.0 / count.astype(jnp.float32)
    for part in range(2):
        for half in range(2):
            rows_ref[4 * half + 3, pl.ds(6 + part, devices, stride=8), :] = jnp.zeros((devices, 128), jnp.float32)
    dft_ref[...] = dft_rows()
    for w in range(windows):
        copies[w].wait()
        spectra = dot(dft_ref[...], records_ref[w], 1, 0)
        real_part = spectra[:BINS]
        imag_part = spectra[BINS:]
        power = real_part * real_part + imag_part * imag_part
        size = jnp.sqrt(power)
        high = size.astype(jnp.bfloat16)
        low = (size - high.astype(jnp.float32)).astype(jnp.bfloat16)
        smooth = (dot(near, high, 1, 0) + dot(near, low, 1, 0)) * weight
        level = jnp.sqrt(jnp.sum(power, axis=0, keepdims=True) * (1.0 / BINS) + 1e-06)
        scale = 1.0 / (smooth + 0.25 * level)
        for part, values in enumerate((real_part * scale, imag_part * scale)):
            for n in range(channels // 128):
                piece = values[:, n * 128 : (n + 1) * 128]
                rows_ref[n, pl.ds(part * 2 + w, devices, stride=8), :] = piece[:devices]
                rows_ref[n, pl.ds(w * 8 + 4 + part, devices // 2, stride=16), :] = piece[devices : BINS - GROUP]
            last = values[BINS - GROUP :]
            last = jnp.concatenate([last, jnp.zeros((GROUP, REACH), jnp.float32)], axis=1)
            for g in range(devices // GROUP):
                begin = g * (channels * GROUP // devices)
                reach = last[:, begin : begin + REACH]
                for n in range(REACH // 128):
                    where = pl.ds(g * GROUP * 8 + 6 + part, GROUP, stride=8)
                    rows_ref[4 * w + n, where, :] = reach[:, n * 128 : (n + 1) * 128]
    for n in range(channels // 128):
        out_ref[:, n * 128 : (n + 1) * 128] = rows_ref[n].astype(jnp.bfloat16)


def whiten(records, devices):
    windows, samples, channels = records.shape
    rows = devices * 8
    return pl.pallas_call(
        functools.partial(whiten_kernel, devices),
        in_specs=[pl.BlockSpec(memory_space=pltpu.HBM)],
        out_specs=pl.BlockSpec(memory_space=pltpu.VMEM),
        out_shape=jax.ShapeDtypeStruct((rows, channels), jnp.bfloat16),
        scratch_shapes=[
            pltpu.VMEM(records.shape, jnp.bfloat16),
            pltpu.VMEM((2 * BINS, samples), jnp.bfloat16),
            pltpu.VMEM((channels // 128, rows, 128), jnp.float32),
            pltpu.SemaphoreType.DMA((windows,)),
        ],
        compiler_params=params(50),
        cost_estimate=cost(2 * windows * samples * channels * 2 * BINS, records.size * 2 + rows * channels * 2),
        name="whiten",
    )(records)


def split_rows(even, odd, gap):
    row = lax.broadcasted_iota(jnp.int32, (1, 8, even.shape[2]), 1)
    first = row // gap % 2 == 0
    return jnp.where(first, even, pltpu.roll(odd, gap, 1)), jnp.where(first, pltpu.roll(even, 8 - gap, 1), odd)


def compact_kernel(rows_ref, own_ref, shared_ref, last_ref):
    row_count, channels = rows_ref.shape
    block = 256

    def halves(value):
        value = value.reshape(value.shape[0] // 2, 2, 8, block)
        return value[:, 0], value[:, 1]

    for begin in range(0, channels, block):
        now = slice(begin, begin + block)
        wide = rows_ref[:, now].astype(jnp.float32).reshape(row_count // 8, 8, block)
        own, rest = split_rows(*halves(wide), 4)
        shared, last = split_rows(*halves(rest), 2)
        for ref, value, gap in ((own_ref, own, 2), (shared_ref, shared, 1), (last_ref, last, 1)):
            for part, piece in enumerate(split_rows(*halves(value), gap)):
                count = ref.shape[0] // 2
                ref[part * count : (part + 1) * count, now] = piece.reshape(count, block).astype(jnp.bfloat16)


def compact(rows):
    row_count, channels = rows.shape
    shapes = [row_count // 2, row_count // 4, row_count // 4]
    return pl.pallas_call(
        compact_kernel,
        out_shape=[jax.ShapeDtypeStruct((n, channels), jnp.bfloat16) for n in shapes],
        in_specs=[pl.BlockSpec(memory_space=pltpu.VMEM)],
        out_specs=[pl.BlockSpec(memory_space=pltpu.VMEM)] * 3,
        compiler_params=params(16),
        cost_estimate=cost(0, 4 * 1024 * 1024),
        name="compact",
    )(rows)


def flip_matrix(count, width):
    row = lax.broadcasted_iota(jnp.int32, (count, width), 0)
    column = lax.broadcasted_iota(jnp.int32, (count, width), 1)
    return jnp.where(row + column == count - 1, 1.0, 0.0).astype(jnp.bfloat16)


def turned(left, width):
    pieces = []
    for begin in range(0, left.shape[1], 2 * width):
        pieces += [left[:, begin + width : begin + 2 * width], -left[:, begin : begin + width]]
    return jnp.concatenate(pieces, axis=1)


def skew_store(part, shift, lane, store):
    second = pltpu.roll(part[:16], (shift + 64) % REACH, 1, stride=1, stride_axis=0)
    first = pltpu.roll(part[16:], (shift + 16) % REACH, 1, stride=1, stride_axis=0)
    for q in range(BAND // 128):
        now = slice(q * 128, (q + 1) * 128)
        then = slice((q + 1) * 128, (q + 2) * 128)
        store(2 * q, jnp.where(lane < 64, first[:, now], second[:, now]).astype(jnp.bfloat16))
        store(2 * q + 1, jnp.where(lane < 64, second[:, then], first[:, now]).astype(jnp.bfloat16))


def store_items(products, c, item, out_ref, lane):
    for i in range(8):
        begin = 128 * (1 - i // 4)
        part = products[i * 32 : (i + 1) * 32, begin : begin + REACH]

        def store(j, value, i=i):
            out_ref[(c * 8 + 7 - i) * 4 + j, item * 16 : (item + 1) * 16, :] = value

        skew_store(part, 257 + 32 * (i % 4), lane, store)


def band_products(left, right_ref, begin, width):
    extent = min(width, right_ref.shape[1] - begin)
    products = dot(left, right_ref[:, begin : begin + extent], 1, 0)
    if extent < width:
        products = jnp.concatenate([products, jnp.zeros((left.shape[0], width - extent), jnp.float32)], axis=1)
    return products


def stack_kernel(info_ref, own_ref, last_ref, out_ref, mine_ref, pair_ref, rest_ref):
    row_count, channels = own_ref.shape
    block = 256
    lane = lax.broadcasted_iota(jnp.int32, (16, 128), 1)
    wide = jnp.concatenate([last_ref[:, :REACH], last_ref[:, 512 : 512 + REACH]], axis=0)
    left = dot(flip_matrix(64, 128), wide[:, :128], 1, 1).astype(jnp.bfloat16)
    left = jnp.concatenate([left, turned(left, row_count // 4)], axis=0)
    products = dot(left, wide, 1, 0)
    for p in range(2):
        for i in range(2):

            def store(j, value, p=p, i=i):
                rest_ref[jnp.where(info_ref[1] == 1 - i, 0, 1), j, p * 16 : (p + 1) * 16, :] = value

            r = p * 64 + i * 32
            skew_store(products[r : r + 32], REACH - 63 + 32 * i, lane, store)
    mine_ref[...] = rest_ref[0]
    pair_ref[...] = rest_ref[1]
    flip = flip_matrix(block, block)
    for c in range(channels // block):
        left = dot(flip, own_ref[:, c * block : (c + 1) * block], 1, 1).astype(jnp.bfloat16)
        left = jnp.concatenate([left, turned(left, row_count // 2)], axis=0)
        products = band_products(left, own_ref, c * block, 2 * block)
        for p in range(2):
            store_items(products[p * block : (p + 1) * block], c, p, out_ref, lane)


def stack(info, own, last, devices):
    shapes = [(devices, 32, 128), (4, 32, 128), (4, 32, 128)]
    return pl.pallas_call(
        stack_kernel,
        out_shape=[jax.ShapeDtypeStruct(shape, jnp.bfloat16) for shape in shapes],
        in_specs=[pl.BlockSpec(memory_space=pltpu.SMEM)] + [pl.BlockSpec(memory_space=pltpu.VMEM)] * 2,
        out_specs=[pl.BlockSpec(memory_space=pltpu.VMEM)] * 3,
        scratch_shapes=[pltpu.VMEM((2, 4, 32, 128), jnp.bfloat16)],
        compiler_params=params(16),
        cost_estimate=cost(4 * 1024 * 512 * 512, 4 * 1024 * 1024),
        name="stack",
    )(info, own, last)


def shared_kernel(info_ref, own_ref, other_ref, items_ref, out_hbm, both_ref, item_ref, sems):
    row_count, channels = own_ref.shape
    block = 256
    copies = [pltpu.make_async_copy(items_ref, out_hbm.at[:, pl.ds(0, 32)], sems.at[0])]
    copies[0].start()
    lane = lax.broadcasted_iota(jnp.int32, (16, 128), 1)
    both_ref[:row_count] = own_ref[...]
    both_ref[row_count:] = other_ref[...]
    core = info_ref[0]
    flip = flip_matrix(block, block)
    for c in range(channels // block):
        left = dot(flip, both_ref[:, c * block : (c + 1) * block], 1, 1).astype(jnp.bfloat16)
        left = jnp.where(core == 0, left, turned(left, row_count // 2))
        products = band_products(left, both_ref, c * block, 2 * block)
        store_items(products, c, 0, item_ref, lane)
        where = pl.ds(c * 32, 32)
        copies.append(
            pltpu.make_async_copy(item_ref.at[where], out_hbm.at[where, pl.ds(32, 16)], sems.at[c + 1])
        )
        copies[-1].start()
    for copy in copies:
        copy.wait()


def stack_shared(info, own, other, items, devices):
    row_count, channels = own.shape
    return pl.pallas_call(
        shared_kernel,
        out_shape=jax.ShapeDtypeStruct((devices, 48, 128), jnp.bfloat16),
        in_specs=[pl.BlockSpec(memory_space=pltpu.SMEM)] + [pl.BlockSpec(memory_space=pltpu.VMEM)] * 3,
        out_specs=pl.BlockSpec(memory_space=pltpu.HBM),
        scratch_shapes=[
            pltpu.VMEM((2 * row_count, channels), jnp.bfloat16),
            pltpu.VMEM((devices, 16, 128), jnp.bfloat16),
            pltpu.SemaphoreType.DMA((1 + channels // 256,)),
        ],
        compiler_params=params(16),
        cost_estimate=cost(2 * 1024 * 512 * 512, 4 * 1024 * 1024),
        name="stack_shared",
    )(info, own, other, items)


def lag_kernel(parts, info_ref, table_ref, stacks_ref, mine_ref, pair_ref, out_hbm, wide_ref, out_ref, sems):
    items = table_ref.shape[0]
    each = 16 // parts
    split = stacks_ref.shape[0]
    wide_ref[:split] = stacks_ref[...].astype(jnp.float32)
    mine, win = info_ref[1], info_ref[2]
    for half, ref in ((mine, mine_ref), (1 - mine, pair_ref)):
        for n in range(4):
            begin = pl.multiple_of(split + (half * 4 + n) * 32, 32)
            wide_ref[pl.ds(begin, 32), :] = ref[n, win].astype(jnp.float32)
    swap = info_ref[0]
    copies = []
    for part in range(parts):
        sides = []
        for n in range(each):
            place = 15 - (part * each + n)
            sides.append(wide_ref[pl.ds(place, items, stride=16), :].astype(jnp.bfloat16))
        both = dot(jnp.concatenate(sides, axis=1), table_ref[...], 0, 0)
        lags = both[:, :LAGS] + both[:, LAGS:]
        for n in range(each):
            for h in range(2):
                r = n * 128 + h * 64
                out_ref[(h + swap) % 2, part * each + n] = lags[r : r + 64]
        where = (slice(None), pl.ds(part * each, each))
        copies.append(pltpu.make_async_copy(out_ref.at[where], out_hbm.at[where], sems.at[part]))
        copies[-1].start()
    for copy in copies:
        copy.wait()


def lag_transform(info, stacks, mine, pair, devices):
    parts = 8
    table = jnp.asarray(lag_rows(devices))
    shape = (2, 16, 64, LAGS)
    out = pl.pallas_call(
        functools.partial(lag_kernel, parts),
        in_specs=[pl.BlockSpec(memory_space=pltpu.SMEM)] + [pl.BlockSpec(memory_space=pltpu.VMEM)] * 4,
        out_specs=pl.BlockSpec(memory_space=pltpu.HBM),
        out_shape=jax.ShapeDtypeStruct(shape, jnp.float32),
        scratch_shapes=[
            pltpu.VMEM((2 * BINS * 16, 128), jnp.float32),
            pltpu.VMEM(shape, jnp.float32),
            pltpu.SemaphoreType.DMA((parts,)),
        ],
        compiler_params=params(24),
        cost_estimate=cost(4 * 2 * BINS * 2048 * 256, 4 * 1024 * 1024),
        name="lag_transform",
    )(info, table, stacks, mine, pair)
    return out.reshape(32, 64, LAGS)


def per_device(chan_size, win_size, records):
    devices = chan_size * win_size
    axes = ("chan", "win")
    channels = records.shape[2]

    def exchange(array):
        return lax.all_to_all(array, axes, split_axis=0, concat_axis=0, tiled=True)

    win = lax.axis_index("win")
    info = jnp.stack([win % 2, lax.axis_index("chan") % 2, win]).astype(jnp.int32)
    rows = whiten(records, devices).reshape(devices, 8, channels)
    rows, info = lax.optimization_barrier((rows, info))
    own, shared, last = compact(exchange(rows).reshape(devices * 8, channels))
    other = lax.ppermute(shared, "win", [(w, w ^ 1) for w in range(win_size)])
    items, mine, pair = stack(info, own, last, devices)
    pair = lax.ppermute(pair, "chan", [(c, c ^ 1) for c in range(chan_size)])
    mine = lax.all_gather(mine, "win")
    pair = lax.all_gather(pair, "win")
    stacks = exchange(stack_shared(info, shared, other, items, devices))
    return lag_transform(info, stacks.reshape(devices * 48, 128), mine, pair, devices)


def solution(mesh):
    in_specs = (P(("chan", "win"), None, None),)
    out_specs = P("chan", "win", None)
    body = functools.partial(per_device, mesh.shape["chan"], mesh.shape["win"])
    return jax.shard_map(body, mesh=mesh, in_specs=in_specs, out_specs=out_specs, check_vma=False)
```

```python
import functools
import math

import jax
import jax.numpy as jnp
import ml_dtypes
import numpy as np
from jax import lax
from jax.experimental import pallas as pl
from jax.experimental.pallas import tpu as pltpu
from jax.sharding import PartitionSpec as P

SAMPLES = 1000
BINS = 200
FIRST_BIN = 20
BAND = 256
LAGS = 256
WINDOWS = 256
GROUP = 8
REACH = 384
LANES = 896


def cos_sin(freqs, times):
    turns = freqs * times
    turns = turns - SAMPLES * jnp.floor(turns * (1.0 / SAMPLES) + 0.5)
    phase = turns * (2.0 * math.pi / SAMPLES)
    return jnp.cos(phase), jnp.sin(phase)


def dft_rows():
    def ramp(rows, axis):
        return lax.broadcasted_iota(jnp.int32, (rows, SAMPLES), axis).astype(jnp.float32)

    near_cos, near_sin = cos_sin(ramp(8, 0), ramp(8, 1))
    base_cos, base_sin = cos_sin(FIRST_BIN + 8.0 * ramp(32, 0), ramp(32, 1))
    real_rows, imag_rows = [], []
    for n in range(BINS // 8):
        far_cos, far_sin = base_cos[n : n + 1], base_sin[n : n + 1]
        real_rows.append(far_cos * near_cos - far_sin * near_sin)
        imag_rows.append(-far_sin * near_cos - far_cos * near_sin)
    return jnp.concatenate(real_rows + imag_rows, axis=0).astype(jnp.bfloat16)


def lag_rows(devices):
    owner = np.arange(devices)
    third = devices + owner // 2
    bins = np.stack([owner, owner, third], axis=1).reshape(-1)
    part = np.stack([0 * owner, 0 * owner + 1, owner % 2], axis=1).reshape(-1)
    last = np.arange(BINS - GROUP, BINS)
    bins = np.concatenate([bins, np.repeat(last, 2)])
    part = np.concatenate([part, np.tile([0, 1], GROUP)])
    shifts = np.arange(LAGS) - LAGS // 2
    phase = ((FIRST_BIN + bins)[:, None] * shifts[None, :] % SAMPLES) * (2.0 * math.pi / SAMPLES)
    table = np.where(part[:, None] == 0, np.cos(phase), -np.sin(phase)) / (WINDOWS * math.sqrt(BINS))
    high = table.astype(ml_dtypes.bfloat16)
    low = (table - high.astype(np.float64)).astype(ml_dtypes.bfloat16)
    return np.concatenate([high, low], axis=1)


def dot(left, right, left_dim, right_dim):
    dims = (((left_dim,), (right_dim,)), ((), ()))
    return lax.dot_general(left, right, dims, preferred_element_type=jnp.float32)


def params(mebibytes):
    return pltpu.CompilerParams(vmem_limit_bytes=mebibytes * 1024 * 1024)


def cost(flops, bytes_accessed):
    return pl.CostEstimate(flops=flops, bytes_accessed=bytes_accessed, transcendentals=0)


def whiten_kernel(devices, records_hbm, out_ref, records_ref, dft_ref, rows_ref, sems):
    windows, _, channels = records_ref.shape
    copies = []
    for w in range(windows):
        copies.append(pltpu.make_async_copy(records_hbm.at[w], records_ref.at[w], sems.at[w]))
        copies[-1].start()
    row = lax.broadcasted_iota(jnp.int32, (BINS, BINS), 0)
    column = lax.broadcasted_iota(jnp.int32, (BINS, BINS), 1)
    near = jnp.where(jnp.abs(row - column) <= 4, 1.0, 0.0).astype(jnp.bfloat16)
    place = lax.broadcasted_iota(jnp.int32, (BINS, 1), 0)
    count = jnp.minimum(place + 4, BINS - 1) - jnp.maximum(place - 4, 0) + 1
    weight = 1.0 / count.astype(jnp.float32)
    for r in (6, 7):
        rows_ref[6, pl.ds(r, devices, stride=8), :] = jnp.zeros((devices, 128), jnp.float32)
    dft_ref[...] = dft_rows()
    for w in range(windows):
        copies[w].wait()
        spectra = dot(dft_ref[...], records_ref[w], 1, 0)
        real_part = spectra[:BINS]
        imag_part = spectra[BINS:]
        power = real_part * real_part + imag_part * imag_part
        size = jnp.sqrt(power)
        high = size.astype(jnp.bfloat16)
        low = (size - high.astype(jnp.float32)).astype(jnp.bfloat16)
        smooth = (dot(near, high, 1, 0) + dot(near, low, 1, 0)) * weight
        level = jnp.sqrt(jnp.sum(power, axis=0, keepdims=True) * (1.0 / BINS) + 1e-06)
        scale = 1.0 / (smooth + 0.25 * level)
        for part, values in enumerate((real_part * scale, imag_part * scale)):
            for n in range(channels // 128):
                piece = values[:, n * 128 : (n + 1) * 128]
                place = pl.ds(n // 4 * 4 + part * 2 + w, devices, stride=8)
                rows_ref[n % 4, place, :] = piece[:devices]
                place = pl.ds(w * 8 + n // 2 * 2 + part, devices // 2, stride=16)
                rows_ref[4 + n % 2, place, :] = piece[devices : BINS - GROUP]
            last = values[BINS - GROUP :]
            last = jnp.concatenate([last, jnp.zeros((GROUP, REACH - 128), jnp.float32)], axis=1)
            for g in range(devices // (2 * GROUP)):
                for n in range(REACH // 128):
                    place = pl.ds(g * 16 * GROUP + w * 8 + n * 2 + part, GROUP, stride=16)
                    rows_ref[6, place, :] = last[:, (g + n) * 128 : (g + n + 1) * 128]
    for n in range(rows_ref.shape[0]):
        out_ref[:, n * 128 : (n + 1) * 128] = rows_ref[n].astype(jnp.bfloat16)


def whiten(records, devices):
    windows, samples, channels = records.shape
    rows = devices * 8
    return pl.pallas_call(
        functools.partial(whiten_kernel, devices),
        in_specs=[pl.BlockSpec(memory_space=pltpu.HBM)],
        out_specs=pl.BlockSpec(memory_space=pltpu.VMEM),
        out_shape=jax.ShapeDtypeStruct((rows, LANES), jnp.bfloat16),
        scratch_shapes=[
            pltpu.VMEM(records.shape, jnp.bfloat16),
            pltpu.VMEM((2 * BINS, samples), jnp.bfloat16),
            pltpu.VMEM((LANES // 128, rows, 128), jnp.float32),
            pltpu.SemaphoreType.DMA((windows,)),
        ],
        compiler_params=params(50),
        cost_estimate=cost(2 * windows * samples * channels * 2 * BINS, records.size * 2 + rows * channels * 2),
        name="whiten",
    )(records)


def split_rows(even, odd, gap):
    row = lax.broadcasted_iota(jnp.int32, (1, 8, even.shape[2]), 1)
    first = row // gap % 2 == 0
    return jnp.where(first, even, pltpu.roll(odd, gap, 1)), jnp.where(first, pltpu.roll(even, 8 - gap, 1), odd)


def flip_matrix(count, width):
    row = lax.broadcasted_iota(jnp.int32, (count, width), 0)
    column = lax.broadcasted_iota(jnp.int32, (count, width), 1)
    return jnp.where(row + column == count - 1, 1.0, 0.0).astype(jnp.bfloat16)


def turned(left, width):
    pieces = []
    for begin in range(0, left.shape[1], 2 * width):
        pieces += [left[:, begin + width : begin + 2 * width], -left[:, begin : begin + width]]
    return jnp.concatenate(pieces, axis=1)


def skew_store(part, shift, lane, store):
    second = pltpu.roll(part[:16], (shift + 64) % REACH, 1, stride=1, stride_axis=0)
    first = pltpu.roll(part[16:], (shift + 16) % REACH, 1, stride=1, stride_axis=0)
    for q in range(BAND // 128):
        now = slice(q * 128, (q + 1) * 128)
        then = slice((q + 1) * 128, (q + 2) * 128)
        store(2 * q, jnp.where(lane < 64, first[:, now], second[:, now]).astype(jnp.bfloat16))
        store(2 * q + 1, jnp.where(lane < 64, second[:, then], first[:, now]).astype(jnp.bfloat16))


def store_items(products, c, item, out_ref, lane):
    for i in range(8):
        begin = 128 * (1 - i // 4)
        part = products[i * 32 : (i + 1) * 32, begin : begin + REACH]

        def store(j, value, i=i):
            out_ref[(c * 8 + 7 - i) * 4 + j, item * 16 : (item + 1) * 16, :] = value

        skew_store(part, 257 + 32 * (i % 4), lane, store)


def band_products(left, right_ref, begin, width, channels):
    extent = min(width, channels - begin)
    products = dot(left, right_ref[:, begin : begin + extent], 1, 0)
    if extent < width:
        products = jnp.concatenate([products, jnp.zeros((left.shape[0], width - extent), jnp.float32)], axis=1)
    return products


def compact_kernel(rows_ref, own_ref, shared_ref):
    row_count = rows_ref.shape[0]
    channels = own_ref.shape[1]

    def halves(value):
        value = value.reshape(value.shape[0] // 2, 2, 8, value.shape[2])
        return value[:, 0], value[:, 1]

    def load(begin, width):
        return rows_ref[:, begin : begin + width].astype(jnp.float32).reshape(row_count // 8, 8, width)

    def store(ref, value, gap, begin):
        count, width = ref.shape[0] // 2, value.shape[2]
        for part, piece in enumerate(split_rows(*halves(value), gap)):
            where = slice(part * count, (part + 1) * count)
            ref[where, begin : begin + width] = piece.reshape(count, width).astype(jnp.bfloat16)

    for begin, width, target in ((512, 256, 0), (768, 128, channels)):
        quarter = 0
        for value in split_rows(*halves(load(begin, width)), 4):
            for piece in split_rows(*halves(value), 2):
                if target + quarter * width < shared_ref.shape[1]:
                    store(shared_ref, piece, 1, target + quarter * width)
                quarter += 1
    for begin in (0, 256):
        for h, value in enumerate(split_rows(*halves(load(begin, 256)), 4)):
            store(own_ref, value, 2, h * 512 + begin)


def compact(rows, channels):
    row_count = rows.shape[0]
    shapes = [(row_count // 2, channels), (row_count // 4, channels + REACH)]
    return pl.pallas_call(
        compact_kernel,
        out_shape=[jax.ShapeDtypeStruct(shape, jnp.bfloat16) for shape in shapes],
        in_specs=[pl.BlockSpec(memory_space=pltpu.VMEM)],
        out_specs=[pl.BlockSpec(memory_space=pltpu.VMEM)] * 2,
        compiler_params=params(16),
        cost_estimate=cost(0, 4 * 1024 * 1024),
        name="compact",
    )(rows)


def stack_kernel(own_ref, out_ref):
    row_count, channels = own_ref.shape
    block = 256
    lane = lax.broadcasted_iota(jnp.int32, (16, 128), 1)
    flip = flip_matrix(block, block)
    for c in range(channels // block):
        left = dot(flip, own_ref[:, c * block : (c + 1) * block], 1, 1).astype(jnp.bfloat16)
        left = jnp.concatenate([left, turned(left, row_count // 2)], axis=0)
        products = band_products(left, own_ref, c * block, 2 * block, channels)
        for p in range(2):
            store_items(products[p * block : (p + 1) * block], c, p, out_ref, lane)


def stack(own, devices):
    return pl.pallas_call(
        stack_kernel,
        out_shape=jax.ShapeDtypeStruct((devices, 32, 128), jnp.bfloat16),
        in_specs=[pl.BlockSpec(memory_space=pltpu.VMEM)],
        out_specs=pl.BlockSpec(memory_space=pltpu.VMEM),
        compiler_params=params(16),
        cost_estimate=cost(4 * 1024 * 512 * 512, 4 * 1024 * 1024),
        name="stack",
    )(own)


def shared_kernel(info_ref, own_ref, other_ref, items_ref, out_hbm, *refs):
    rest_refs, (both_ref, item_ref, rest_ref, sems) = refs[:4], refs[4:]
    row_count, width = own_ref.shape
    channels = width - REACH
    block = 256
    copies = [pltpu.make_async_copy(items_ref, out_hbm.at[:, pl.ds(0, 32)], sems.at[0])]
    copies[0].start()
    lane = lax.broadcasted_iota(jnp.int32, (16, 128), 1)
    both_ref[:row_count] = own_ref[...]
    both_ref[row_count:] = other_ref[...]
    core = info_ref[0]

    def left_side(flip, begin):
        left = dot(flip, both_ref[:, begin : begin + flip.shape[0]], 1, 1).astype(jnp.bfloat16)
        return jnp.where(core == 0, left, turned(left, row_count // 2))

    flip = flip_matrix(block, block)
    for c in range(channels // block):
        products = band_products(left_side(flip, c * block), both_ref, c * block, 2 * block, channels)
        store_items(products, c, 0, item_ref, lane)
        where = pl.ds(c * 32, 32)
        copies.append(
            pltpu.make_async_copy(item_ref.at[where], out_hbm.at[where, pl.ds(32, 16)], sems.at[c + 1])
        )
        copies[-1].start()
    products = dot(left_side(flip_matrix(128, 128), channels), both_ref[:, channels:], 1, 0)
    for i in range(4):

        def store(j, value, i=i):
            rest_ref[jnp.bitwise_and(7 - i - info_ref[1], 3), j] = value

        skew_store(products[i * 32 : (i + 1) * 32], 257 + 32 * i, lane, store)
    for n, ref in enumerate(rest_refs):
        ref[...] = rest_ref[n]
    for copy in copies:
        copy.wait()


def stack_shared(info, own, other, items, devices):
    row_count, width = own.shape
    shapes = [(devices, 48, 128)] + [(4, 16, 128)] * 4
    return pl.pallas_call(
        shared_kernel,
        out_shape=[jax.ShapeDtypeStruct(shape, jnp.bfloat16) for shape in shapes],
        in_specs=[pl.BlockSpec(memory_space=pltpu.SMEM)] + [pl.BlockSpec(memory_space=pltpu.VMEM)] * 3,
        out_specs=[pl.BlockSpec(memory_space=pltpu.HBM)] + [pl.BlockSpec(memory_space=pltpu.VMEM)] * 4,
        scratch_shapes=[
            pltpu.VMEM((2 * row_count, width), jnp.bfloat16),
            pltpu.VMEM((devices, 16, 128), jnp.bfloat16),
            pltpu.VMEM((4, 4, 16, 128), jnp.bfloat16),
            pltpu.SemaphoreType.DMA((1 + (width - REACH) // 256,)),
        ],
        compiler_params=params(16),
        cost_estimate=cost(2 * 1024 * 512 * 512, 4 * 1024 * 1024),
        name="stack_shared",
    )(info, own, other, items)


def lag_kernel(parts, info_ref, table_ref, stacks_ref, rest_ref, out_hbm, wide_ref, out_ref, sems):
    items = table_ref.shape[0]
    each = 16 // parts
    split = stacks_ref.shape[0]
    wide_ref[:split] = stacks_ref[...].astype(jnp.float32)
    for k in range(4):
        source = jnp.bitwise_and(info_ref[1] + 4 - k, 3)
        for n in range(4):
            begin = pl.multiple_of(split + (source * 4 + n) * 16, 16)
            wide_ref[pl.ds(begin, 16), :] = rest_ref[n, k * 4 + info_ref[2]].astype(jnp.float32)
    swap = info_ref[0]
    copies = []
    for part in range(parts):
        sides = []
        for n in range(each):
            place = 15 - (part * each + n)
            sides.append(wide_ref[pl.ds(place, items, stride=16), :].astype(jnp.bfloat16))
        both = dot(jnp.concatenate(sides, axis=1), table_ref[...], 0, 0)
        lags = both[:, :LAGS] + both[:, LAGS:]
        for n in range(each):
            for h in range(2):
                r = n * 128 + h * 64
                out_ref[(h + swap) % 2, part * each + n] = lags[r : r + 64]
        where = (slice(None), pl.ds(part * each, each))
        copies.append(pltpu.make_async_copy(out_ref.at[where], out_hbm.at[where], sems.at[part]))
        copies[-1].start()
    for copy in copies:
        copy.wait()


def lag_transform(info, stacks, rest, devices):
    parts = 8
    table = jnp.asarray(lag_rows(devices))
    shape = (2, 16, 64, LAGS)
    out = pl.pallas_call(
        functools.partial(lag_kernel, parts),
        in_specs=[pl.BlockSpec(memory_space=pltpu.SMEM)] + [pl.BlockSpec(memory_space=pltpu.VMEM)] * 3,
        out_specs=pl.BlockSpec(memory_space=pltpu.HBM),
        out_shape=jax.ShapeDtypeStruct(shape, jnp.float32),
        scratch_shapes=[
            pltpu.VMEM((2 * BINS * 16, 128), jnp.float32),
            pltpu.VMEM(shape, jnp.float32),
            pltpu.SemaphoreType.DMA((parts,)),
        ],
        compiler_params=params(24),
        cost_estimate=cost(4 * 2 * BINS * 2048 * 256, 4 * 1024 * 1024),
        name="lag_transform",
    )(info, table, stacks, rest)
    return out.reshape(32, 64, LAGS)


def per_device(chan_size, win_size, records):
    devices = chan_size * win_size
    axes = ("chan", "win")
    channels = records.shape[2]

    def exchange(array):
        return lax.all_to_all(array, axes, split_axis=0, concat_axis=0, tiled=True)

    chan, win = lax.axis_index("chan"), lax.axis_index("win")
    info = jnp.stack([win % 2, chan % 4, win]).astype(jnp.int32)
    rows = whiten(records, devices).reshape(devices, 8, LANES)
    rows, info = lax.optimization_barrier((rows, info))
    own, shared = compact(exchange(rows).reshape(devices * 8, LANES), channels)
    other = lax.ppermute(shared, "win", [(w, w ^ 1) for w in range(win_size)])
    items = stack(own, devices)
    stacks, *rest = stack_shared(info, shared, other, items, devices)
    for n in range(1, 4):
        rest[n] = lax.ppermute(rest[n], "chan", [(c, c // 4 * 4 + (c + n) % 4) for c in range(chan_size)])
    rest = lax.all_gather(jnp.concatenate(rest), "win")
    return lag_transform(info, exchange(stacks).reshape(devices * 48, 128), rest, devices)


def solution(mesh):
    in_specs = (P(("chan", "win"), None, None),)
    out_specs = P("chan", "win", None)
    body = functools.partial(per_device, mesh.shape["chan"], mesh.shape["win"])
    return jax.shard_map(body, mesh=mesh, in_specs=in_specs, out_specs=out_specs, check_vma=False)
```

```python
import functools
import math

import jax
import jax.numpy as jnp
import ml_dtypes
import numpy as np
from jax import lax
from jax.experimental import pallas as pl
from jax.experimental.pallas import tpu as pltpu
from jax.sharding import PartitionSpec as P

SAMPLES = 1000
BINS = 200
FIRST_BIN = 20
BAND = 256
LAGS = 256
WINDOWS = 256
GROUP = 8
REACH = 384
LANES = 896


def cos_sin(freqs, times):
    turns = freqs * times
    turns = turns - SAMPLES * jnp.floor(turns * (1.0 / SAMPLES) + 0.5)
    phase = turns * (2.0 * math.pi / SAMPLES)
    return jnp.cos(phase), jnp.sin(phase)


def dft_rows():
    def ramp(rows, axis):
        return lax.broadcasted_iota(jnp.int32, (rows, SAMPLES), axis).astype(jnp.float32)

    near_cos, near_sin = cos_sin(ramp(8, 0), ramp(8, 1))
    base_cos, base_sin = cos_sin(FIRST_BIN + 8.0 * ramp(32, 0), ramp(32, 1))
    real_rows, imag_rows = [], []
    for n in range(BINS // 8):
        far_cos, far_sin = base_cos[n : n + 1], base_sin[n : n + 1]
        real_rows.append(far_cos * near_cos - far_sin * near_sin)
        imag_rows.append(-far_sin * near_cos - far_cos * near_sin)
    return jnp.concatenate(real_rows + imag_rows, axis=0).astype(jnp.bfloat16)


def lag_rows(devices):
    owner = np.arange(devices)
    third = devices + owner // 2
    bins = np.stack([owner, owner, third], axis=1).reshape(-1)
    part = np.stack([0 * owner, 0 * owner + 1, owner % 2], axis=1).reshape(-1)
    last = np.arange(BINS - GROUP, BINS)
    bins = np.concatenate([bins, np.repeat(last, 2)])
    part = np.concatenate([part, np.tile([0, 1], GROUP)])
    shifts = np.arange(LAGS) - LAGS // 2
    phase = ((FIRST_BIN + bins)[:, None] * shifts[None, :] % SAMPLES) * (2.0 * math.pi / SAMPLES)
    table = np.where(part[:, None] == 0, np.cos(phase), -np.sin(phase)) / (WINDOWS * math.sqrt(BINS))
    high = table.astype(ml_dtypes.bfloat16)
    low = (table - high.astype(np.float64)).astype(ml_dtypes.bfloat16)
    return np.concatenate([high, low], axis=1)


def dot(left, right, left_dim, right_dim):
    dims = (((left_dim,), (right_dim,)), ((), ()))
    return lax.dot_general(left, right, dims, preferred_element_type=jnp.float32)


def params(mebibytes):
    return pltpu.CompilerParams(vmem_limit_bytes=mebibytes * 1024 * 1024)


def cost(flops, bytes_accessed):
    return pl.CostEstimate(flops=flops, bytes_accessed=bytes_accessed, transcendentals=0)


def whiten_kernel(devices, records_hbm, out_ref, records_ref, dft_ref, rows_ref, sems):
    windows, _, channels = records_ref.shape
    copies = []
    for w in range(windows):
        copies.append(pltpu.make_async_copy(records_hbm.at[w], records_ref.at[w], sems.at[w]))
        copies[-1].start()
    row = lax.broadcasted_iota(jnp.int32, (BINS, 2 * BINS), 0)
    column = lax.broadcasted_iota(jnp.int32, (BINS, 2 * BINS), 1)
    column = jnp.where(column < BINS, column, column - BINS)
    near = jnp.where(jnp.abs(row - column) <= 4, 1.0, 0.0).astype(jnp.bfloat16)
    place = lax.broadcasted_iota(jnp.int32, (BINS, 1), 0)
    count = jnp.minimum(place + 4, BINS - 1) - jnp.maximum(place - 4, 0) + 1
    weight = 1.0 / count.astype(jnp.float32)
    for r in (6, 7):
        rows_ref[6, pl.ds(r, devices, stride=8), :] = jnp.zeros((devices, 128), jnp.float32)
    dft_ref[...] = dft_rows()
    for w in range(windows):
        copies[w].wait()
        spectra = dot(dft_ref[...], records_ref[w], 1, 0)
        real_part = spectra[:BINS]
        imag_part = spectra[BINS:]
        power = real_part * real_part + imag_part * imag_part
        size = jnp.sqrt(power)
        high = size.astype(jnp.bfloat16).astype(jnp.float32)
        both = jnp.concatenate([high, size - high], axis=0).astype(jnp.bfloat16)
        smooth = dot(near, both, 1, 0) * weight
        level = jnp.sqrt(jnp.sum(power, axis=0, keepdims=True) * (1.0 / BINS) + 1e-06)
        scale = 1.0 / (smooth + 0.25 * level)
        for part, values in enumerate((real_part * scale, imag_part * scale)):
            for n in range(channels // 128):
                piece = values[:, n * 128 : (n + 1) * 128]
                place = pl.ds(n // 4 * 4 + part * 2 + w, devices, stride=8)
                rows_ref[n % 4, place, :] = piece[:devices]
                place = pl.ds(w * 8 + n // 2 * 2 + part, devices // 2, stride=16)
                rows_ref[4 + n % 2, place, :] = piece[devices : BINS - GROUP]
            last = values[BINS - GROUP :]
            last = jnp.concatenate([last, jnp.zeros((GROUP, REACH - 128), jnp.float32)], axis=1)
            for g in range(devices // (2 * GROUP)):
                for n in range(REACH // 128):
                    place = pl.ds(g * 16 * GROUP + w * 8 + n * 2 + part, GROUP, stride=16)
                    rows_ref[6, place, :] = last[:, (g + n) * 128 : (g + n + 1) * 128]
    for n in range(rows_ref.shape[0]):
        out_ref[:, n * 128 : (n + 1) * 128] = rows_ref[n].astype(jnp.bfloat16)


def whiten(records, devices):
    windows, samples, channels = records.shape
    rows = devices * 8
    return pl.pallas_call(
        functools.partial(whiten_kernel, devices),
        in_specs=[pl.BlockSpec(memory_space=pltpu.HBM)],
        out_specs=pl.BlockSpec(memory_space=pltpu.VMEM),
        out_shape=jax.ShapeDtypeStruct((rows, LANES), jnp.bfloat16),
        scratch_shapes=[
            pltpu.VMEM(records.shape, jnp.bfloat16),
            pltpu.VMEM((2 * BINS, samples), jnp.bfloat16),
            pltpu.VMEM((LANES // 128, rows, 128), jnp.float32),
            pltpu.SemaphoreType.DMA((windows,)),
        ],
        compiler_params=params(50),
        cost_estimate=cost(2 * windows * samples * channels * 2 * BINS, records.size * 2 + rows * channels * 2),
        name="whiten",
    )(records)


def split_rows(even, odd, gap):
    row = lax.broadcasted_iota(jnp.int32, (1, 8, even.shape[2]), 1)
    first = row // gap % 2 == 0
    return jnp.where(first, even, pltpu.roll(odd, gap, 1)), jnp.where(first, pltpu.roll(even, 8 - gap, 1), odd)


def flip_matrix(count, width):
    row = lax.broadcasted_iota(jnp.int32, (count, width), 0)
    column = lax.broadcasted_iota(jnp.int32, (count, width), 1)
    return jnp.where(row + column == count - 1, 1.0, 0.0).astype(jnp.bfloat16)


def turned(left, width):
    pieces = []
    for begin in range(0, left.shape[1], 2 * width):
        pieces += [left[:, begin + width : begin + 2 * width], -left[:, begin : begin + width]]
    return jnp.concatenate(pieces, axis=1)


def skew_store(part, shift, lane, store):
    second = pltpu.roll(part[:16], (shift + 64) % REACH, 1, stride=1, stride_axis=0)
    first = pltpu.roll(part[16:], (shift + 16) % REACH, 1, stride=1, stride_axis=0)
    for q in range(BAND // 128):
        now = slice(q * 128, (q + 1) * 128)
        then = slice((q + 1) * 128, (q + 2) * 128)
        store(2 * q, jnp.where(lane < 64, first[:, now], second[:, now]).astype(jnp.bfloat16))
        store(2 * q + 1, jnp.where(lane < 64, second[:, then], first[:, now]).astype(jnp.bfloat16))


def store_items(products, c, item, out_ref, lane):
    for i in range(8):
        begin = 128 * (1 - i // 4)
        part = products[i * 32 : (i + 1) * 32, begin : begin + REACH]

        def store(j, value, i=i):
            out_ref[(c * 8 + 7 - i) * 4 + j, item * 16 : (item + 1) * 16, :] = value

        skew_store(part, 257 + 32 * (i % 4), lane, store)


def band_products(left, right_ref, begin, width, channels):
    extent = min(width, channels - begin)
    products = dot(left, right_ref[:, begin : begin + extent], 1, 0)
    if extent < width:
        products = jnp.concatenate([products, jnp.zeros((left.shape[0], width - extent), jnp.float32)], axis=1)
    return products


def compact_kernel(rows_ref, own_ref, shared_ref):
    row_count = rows_ref.shape[0]
    channels = own_ref.shape[1]

    def halves(value):
        value = value.reshape(value.shape[0] // 2, 2, 8, value.shape[2])
        return value[:, 0], value[:, 1]

    def load(begin, width):
        return rows_ref[:, begin : begin + width].astype(jnp.float32).reshape(row_count // 8, 8, width)

    def store(ref, value, gap, begin):
        count, width = ref.shape[0] // 2, value.shape[2]
        for part, piece in enumerate(split_rows(*halves(value), gap)):
            where = slice(part * count, (part + 1) * count)
            ref[where, begin : begin + width] = piece.reshape(count, width).astype(jnp.bfloat16)

    for begin, width, target in ((512, 256, 0), (768, 128, channels)):
        quarter = 0
        for value in split_rows(*halves(load(begin, width)), 4):
            for piece in split_rows(*halves(value), 2):
                if target + quarter * width < shared_ref.shape[1]:
                    store(shared_ref, piece, 1, target + quarter * width)
                quarter += 1
    for begin in (0, 256):
        for h, value in enumerate(split_rows(*halves(load(begin, 256)), 4)):
            store(own_ref, value, 2, h * 512 + begin)


def compact(rows, channels):
    row_count = rows.shape[0]
    shapes = [(row_count // 2, channels), (row_count // 4, channels + REACH)]
    return pl.pallas_call(
        compact_kernel,
        out_shape=[jax.ShapeDtypeStruct(shape, jnp.bfloat16) for shape in shapes],
        in_specs=[pl.BlockSpec(memory_space=pltpu.VMEM)],
        out_specs=[pl.BlockSpec(memory_space=pltpu.VMEM)] * 2,
        compiler_params=params(16),
        cost_estimate=cost(0, 4 * 1024 * 1024),
        name="compact",
    )(rows)


def stack_kernel(own_ref, out_ref):
    row_count, channels = own_ref.shape
    block = 256
    lane = lax.broadcasted_iota(jnp.int32, (16, 128), 1)
    flip = flip_matrix(block, block)
    for c in range(channels // block):
        left = dot(flip, own_ref[:, c * block : (c + 1) * block], 1, 1).astype(jnp.bfloat16)
        left = jnp.concatenate([left, turned(left, row_count // 2)], axis=0)
        products = band_products(left, own_ref, c * block, 2 * block, channels)
        for p in range(2):
            store_items(products[p * block : (p + 1) * block], c, p, out_ref, lane)


def stack(own, devices):
    return pl.pallas_call(
        stack_kernel,
        out_shape=jax.ShapeDtypeStruct((devices, 32, 128), jnp.bfloat16),
        in_specs=[pl.BlockSpec(memory_space=pltpu.VMEM)],
        out_specs=pl.BlockSpec(memory_space=pltpu.VMEM),
        compiler_params=params(16),
        cost_estimate=cost(4 * 1024 * 512 * 512, 4 * 1024 * 1024),
        name="stack",
    )(own)


def shared_kernel(info_ref, own_ref, other_ref, items_ref, out_hbm, *refs):
    rest_refs, (both_ref, item_ref, rest_ref, sems) = refs[:4], refs[4:]
    row_count, width = own_ref.shape
    channels = width - REACH
    block = 256
    copies = [pltpu.make_async_copy(items_ref, out_hbm.at[:, pl.ds(0, 32)], sems.at[0])]
    copies[0].start()
    lane = lax.broadcasted_iota(jnp.int32, (16, 128), 1)
    both_ref[:row_count] = own_ref[...]
    both_ref[row_count:] = other_ref[...]
    core = info_ref[0]

    def left_side(flip, begin):
        left = dot(flip, both_ref[:, begin : begin + flip.shape[0]], 1, 1).astype(jnp.bfloat16)
        return jnp.where(core == 0, left, turned(left, row_count // 2))

    flip = flip_matrix(block, block)
    for c in range(channels // block):
        products = band_products(left_side(flip, c * block), both_ref, c * block, 2 * block, channels)
        store_items(products, c, 0, item_ref, lane)
        where = pl.ds(c * 32, 32)
        copies.append(
            pltpu.make_async_copy(item_ref.at[where], out_hbm.at[where, pl.ds(32, 16)], sems.at[c + 1])
        )
        copies[-1].start()
    products = dot(left_side(flip_matrix(128, 128), channels), both_ref[:, channels:], 1, 0)
    for i in range(4):

        def store(j, value, i=i):
            rest_ref[jnp.bitwise_and(7 - i - info_ref[1], 3), j] = value

        skew_store(products[i * 32 : (i + 1) * 32], 257 + 32 * i, lane, store)
    for n, ref in enumerate(rest_refs):
        ref[...] = rest_ref[n]
    for copy in copies:
        copy.wait()


def stack_shared(info, own, other, items, devices):
    row_count, width = own.shape
    shapes = [(devices, 48, 128)] + [(4, 16, 128)] * 4
    return pl.pallas_call(
        shared_kernel,
        out_shape=[jax.ShapeDtypeStruct(shape, jnp.bfloat16) for shape in shapes],
        in_specs=[pl.BlockSpec(memory_space=pltpu.SMEM)] + [pl.BlockSpec(memory_space=pltpu.VMEM)] * 3,
        out_specs=[pl.BlockSpec(memory_space=pltpu.HBM)] + [pl.BlockSpec(memory_space=pltpu.VMEM)] * 4,
        scratch_shapes=[
            pltpu.VMEM((2 * row_count, width), jnp.bfloat16),
            pltpu.VMEM((devices, 16, 128), jnp.bfloat16),
            pltpu.VMEM((4, 4, 16, 128), jnp.bfloat16),
            pltpu.SemaphoreType.DMA((1 + (width - REACH) // 256,)),
        ],
        compiler_params=params(16),
        cost_estimate=cost(2 * 1024 * 512 * 512, 4 * 1024 * 1024),
        name="stack_shared",
    )(info, own, other, items)


def lag_kernel(parts, info_ref, table_ref, stacks_ref, rest_ref, out_hbm, wide_ref, last_ref, out_ref, sems):
    each = 16 // parts
    split = stacks_ref.shape[0]
    wide_ref[...] = stacks_ref[...].astype(jnp.float32)
    for k in range(4):
        source = jnp.bitwise_and(info_ref[1] + 4 - k, 3)
        for n in range(4):
            begin = pl.multiple_of((source * 4 + n) * 16, 16)
            last_ref[pl.ds(begin, 16), :] = rest_ref[n, k * 4 + info_ref[2]].astype(jnp.float32)
    swap = info_ref[0]
    copies = []
    for part in range(parts):
        sides = []
        for n in range(each):
            place = 15 - (part * each + n)
            side = [wide_ref[pl.ds(place, split // 16, stride=16), :], last_ref[pl.ds(place, 16, stride=16), :]]
            sides.append(jnp.concatenate(side, axis=0).astype(jnp.bfloat16))
        both = dot(jnp.concatenate(sides, axis=1), table_ref[...], 0, 0)
        lags = both[:, :LAGS] + both[:, LAGS:]
        for n in range(each):
            for h in range(2):
                r = n * 128 + h * 64
                out_ref[(h + swap) % 2, part * each + n] = lags[r : r + 64]
        where = (slice(None), pl.ds(part * each, each))
        copies.append(pltpu.make_async_copy(out_ref.at[where], out_hbm.at[where], sems.at[part]))
        copies[-1].start()
    for copy in copies:
        copy.wait()


def lag_transform(info, stacks, rest, devices):
    parts = 8
    table = jnp.asarray(lag_rows(devices))
    shape = (2, 16, 64, LAGS)
    out = pl.pallas_call(
        functools.partial(lag_kernel, parts),
        in_specs=[pl.BlockSpec(memory_space=pltpu.SMEM)] + [pl.BlockSpec(memory_space=pltpu.VMEM)] * 3,
        out_specs=pl.BlockSpec(memory_space=pltpu.HBM),
        out_shape=jax.ShapeDtypeStruct(shape, jnp.float32),
        scratch_shapes=[
            pltpu.VMEM(stacks.shape, jnp.float32),
            pltpu.VMEM((2 * GROUP * 16, 128), jnp.float32),
            pltpu.VMEM(shape, jnp.float32),
            pltpu.SemaphoreType.DMA((parts,)),
        ],
        compiler_params=params(24),
        cost_estimate=cost(4 * 2 * BINS * 2048 * 256, 4 * 1024 * 1024),
        name="lag_transform",
    )(info, table, stacks, rest)
    return out.reshape(32, 64, LAGS)


def per_device(chan_size, win_size, records):
    devices = chan_size * win_size
    axes = ("chan", "win")
    channels = records.shape[2]

    def exchange(array):
        return lax.all_to_all(array, axes, split_axis=0, concat_axis=0, tiled=True)

    chan, win = lax.axis_index("chan"), lax.axis_index("win")
    info = jnp.stack([win % 2, chan % 4, win]).astype(jnp.int32)
    rows = whiten(records, devices).reshape(devices, 8, LANES)
    rows, info = lax.optimization_barrier((rows, info))
    own, shared = compact(exchange(rows).reshape(devices * 8, LANES), channels)
    other = lax.ppermute(shared, "win", [(w, w ^ 1) for w in range(win_size)])
    items = stack(own, devices)
    stacks, *rest = stack_shared(info, shared, other, items, devices)
    for n in range(1, 4):
        rest[n] = lax.ppermute(rest[n], "chan", [(c, c // 4 * 4 + (c + n) % 4) for c in range(chan_size)])
    rest = lax.all_gather(jnp.concatenate(rest), "win")
    return lag_transform(info, exchange(stacks).reshape(devices * 48, 128), rest, devices)


def solution(mesh):
    in_specs = (P(("chan", "win"), None, None),)
    out_specs = P("chan", "win", None)
    body = functools.partial(per_device, mesh.shape["chan"], mesh.shape["win"])
    return jax.shard_map(body, mesh=mesh, in_specs=in_specs, out_specs=out_specs, check_vma=False)
```

```python
import functools
import math

import jax
import jax.numpy as jnp
import ml_dtypes
import numpy as np
from jax import lax
from jax.experimental import pallas as pl
from jax.experimental.pallas import tpu as pltpu
from jax.sharding import PartitionSpec as P

SAMPLES = 1000
BINS = 200
FIRST_BIN = 20
BAND = 256
LAGS = 256
WINDOWS = 256
GROUP = 8
REACH = 384
LANES = 896


def cos_sin(freqs, times):
    turns = freqs * times
    turns = turns - SAMPLES * jnp.floor(turns * (1.0 / SAMPLES) + 0.5)
    phase = turns * (2.0 * math.pi / SAMPLES)
    return jnp.cos(phase), jnp.sin(phase)


def dft_rows():
    def ramp(rows, axis):
        return lax.broadcasted_iota(jnp.int32, (rows, SAMPLES), axis).astype(jnp.float32)

    near_cos, near_sin = cos_sin(ramp(8, 0), ramp(8, 1))
    base_cos, base_sin = cos_sin(FIRST_BIN + 8.0 * ramp(32, 0), ramp(32, 1))
    real_rows, imag_rows = [], []
    for n in range(BINS // 8):
        far_cos, far_sin = base_cos[n : n + 1], base_sin[n : n + 1]
        real_rows.append(far_cos * near_cos - far_sin * near_sin)
        imag_rows.append(-far_sin * near_cos - far_cos * near_sin)
    return jnp.concatenate(real_rows + imag_rows, axis=0).astype(jnp.bfloat16)


def lag_rows(devices):
    owner = np.arange(devices)
    third = devices + owner // 2
    bins = np.stack([owner, owner, third], axis=1).reshape(-1)
    part = np.stack([0 * owner, 0 * owner + 1, owner % 2], axis=1).reshape(-1)
    last = np.arange(BINS - GROUP, BINS)
    bins = np.concatenate([bins, np.repeat(last, 2)])
    part = np.concatenate([part, np.tile([0, 1], GROUP)])
    shifts = np.arange(LAGS) - LAGS // 2
    phase = ((FIRST_BIN + bins)[:, None] * shifts[None, :] % SAMPLES) * (2.0 * math.pi / SAMPLES)
    table = np.where(part[:, None] == 0, np.cos(phase), -np.sin(phase)) / (WINDOWS * math.sqrt(BINS))
    high = table.astype(ml_dtypes.bfloat16)
    low = (table - high.astype(np.float64)).astype(ml_dtypes.bfloat16)
    return np.concatenate([high, low], axis=1)


def dot(left, right, left_dim, right_dim):
    dims = (((left_dim,), (right_dim,)), ((), ()))
    return lax.dot_general(left, right, dims, preferred_element_type=jnp.float32)


def params(mebibytes):
    return pltpu.CompilerParams(vmem_limit_bytes=mebibytes * 1024 * 1024)


def cost(flops, bytes_accessed):
    return pl.CostEstimate(flops=flops, bytes_accessed=bytes_accessed, transcendentals=0)


def whiten_kernel(devices, records_hbm, out_ref, records_ref, dft_ref, rows_ref, sems):
    windows, _, channels = records_ref.shape
    copies = []
    for w in range(windows):
        copies.append(pltpu.make_async_copy(records_hbm.at[w], records_ref.at[w], sems.at[w]))
        copies[-1].start()
    row = lax.broadcasted_iota(jnp.int32, (BINS, 2 * BINS), 0)
    column = lax.broadcasted_iota(jnp.int32, (BINS, 2 * BINS), 1)
    column = jnp.where(column < BINS, column, column - BINS)
    near = jnp.where(jnp.abs(row - column) <= 4, 1.0, 0.0).astype(jnp.bfloat16)
    place = lax.broadcasted_iota(jnp.int32, (BINS, 1), 0)
    count = jnp.minimum(place + 4, BINS - 1) - jnp.maximum(place - 4, 0) + 1
    weight = 1.0 / count.astype(jnp.float32)
    for r in (6, 7):
        rows_ref[6, pl.ds(r, devices, stride=8), :] = jnp.zeros((devices, 128), jnp.float32)
    dft_ref[...] = dft_rows()
    for w in range(windows):
        copies[w].wait()
        spectra = dot(dft_ref[...], records_ref[w], 1, 0)
        real_part = spectra[:BINS]
        imag_part = spectra[BINS:]
        power = real_part * real_part + imag_part * imag_part
        size = jnp.sqrt(power)
        high = size.astype(jnp.bfloat16).astype(jnp.float32)
        both = jnp.concatenate([high, size - high], axis=0).astype(jnp.bfloat16)
        smooth = dot(near, both, 1, 0) * weight
        level = jnp.sqrt(jnp.sum(power, axis=0, keepdims=True) * (1.0 / BINS) + 1e-06)
        scale = 1.0 / (smooth + 0.25 * level)
        for part, values in enumerate((real_part * scale, imag_part * scale)):
            for n in range(channels // 128):
                piece = values[:, n * 128 : (n + 1) * 128]
                place = pl.ds(n // 4 * 4 + part * 2 + w, devices, stride=8)
                rows_ref[n % 4, place, :] = piece[:devices]
                place = pl.ds(w * 8 + n // 2 * 2 + part, devices // 2, stride=16)
                rows_ref[4 + n % 2, place, :] = piece[devices : BINS - GROUP]
            last = values[BINS - GROUP :]
            last = jnp.concatenate([last, jnp.zeros((GROUP, REACH - 128), jnp.float32)], axis=1)
            for g in range(devices // (2 * GROUP)):
                for n in range(REACH // 128):
                    place = pl.ds(g * 16 * GROUP + w * 8 + n * 2 + part, GROUP, stride=16)
                    rows_ref[6, place, :] = last[:, (g + n) * 128 : (g + n + 1) * 128]
    for n in range(rows_ref.shape[0]):
        out_ref[:, n * 128 : (n + 1) * 128] = rows_ref[n].astype(jnp.bfloat16)


def whiten(records, devices):
    windows, samples, channels = records.shape
    rows = devices * 8
    return pl.pallas_call(
        functools.partial(whiten_kernel, devices),
        in_specs=[pl.BlockSpec(memory_space=pltpu.HBM)],
        out_specs=pl.BlockSpec(memory_space=pltpu.VMEM),
        out_shape=jax.ShapeDtypeStruct((rows, LANES), jnp.bfloat16),
        scratch_shapes=[
            pltpu.VMEM(records.shape, jnp.bfloat16),
            pltpu.VMEM((2 * BINS, samples), jnp.bfloat16),
            pltpu.VMEM((LANES // 128, rows, 128), jnp.float32),
            pltpu.SemaphoreType.DMA((windows,)),
        ],
        compiler_params=params(50),
        cost_estimate=cost(2 * windows * samples * channels * 2 * BINS, records.size * 2 + rows * channels * 2),
        name="whiten",
    )(records)


def split_rows(even, odd, gap):
    row = lax.broadcasted_iota(jnp.int32, (1, 8, even.shape[2]), 1)
    first = row // gap % 2 == 0
    return jnp.where(first, even, pltpu.roll(odd, gap, 1)), jnp.where(first, pltpu.roll(even, 8 - gap, 1), odd)


def flip_matrix(count, width):
    row = lax.broadcasted_iota(jnp.int32, (count, width), 0)
    column = lax.broadcasted_iota(jnp.int32, (count, width), 1)
    return jnp.where(row + column == count - 1, 1.0, 0.0).astype(jnp.bfloat16)


def turned(left, width):
    pieces = []
    for begin in range(0, left.shape[1], 2 * width):
        pieces += [left[:, begin + width : begin + 2 * width], -left[:, begin : begin + width]]
    return jnp.concatenate(pieces, axis=1)


def skew_store(part, shift, lane, store):
    second = pltpu.roll(part[:16], (shift + 64) % REACH, 1, stride=1, stride_axis=0)
    first = pltpu.roll(part[16:], (shift + 16) % REACH, 1, stride=1, stride_axis=0)
    for q in range(BAND // 128):
        now = slice(q * 128, (q + 1) * 128)
        then = slice((q + 1) * 128, (q + 2) * 128)
        store(2 * q, jnp.where(lane < 64, first[:, now], second[:, now]).astype(jnp.bfloat16))
        store(2 * q + 1, jnp.where(lane < 64, second[:, then], first[:, now]).astype(jnp.bfloat16))


def store_items(products, c, item, out_ref, lane):
    for i in range(8):
        begin = 128 * (1 - i // 4)
        part = products[i * 32 : (i + 1) * 32, begin : begin + REACH]

        def store(j, value, i=i):
            out_ref[(c * 8 + 7 - i) * 4 + j, item * 16 : (item + 1) * 16, :] = value

        skew_store(part, 257 + 32 * (i % 4), lane, store)


def band_products(left, right_ref, begin, width, channels):
    extent = min(width, channels - begin)
    products = dot(left, right_ref[:, begin : begin + extent], 1, 0)
    if extent < width:
        products = jnp.concatenate([products, jnp.zeros((left.shape[0], width - extent), jnp.float32)], axis=1)
    return products


def halves(value):
    value = value.reshape(value.shape[0] // 2, 2, 8, value.shape[2])
    return value[:, 0], value[:, 1]


def load_rows(rows_ref, begin, width):
    row_count = rows_ref.shape[0]
    return rows_ref[:, begin : begin + width].astype(jnp.float32).reshape(row_count // 8, 8, width)


def store_parts(ref, value, gap, begin):
    count, width = ref.shape[0] // 2, value.shape[2]
    for part, piece in enumerate(split_rows(*halves(value), gap)):
        where = slice(part * count, (part + 1) * count)
        ref[where, begin : begin + width] = piece.reshape(count, width).astype(jnp.bfloat16)


def compact_kernel(channels, rows_ref, shared_ref):
    for begin, width, target in ((512, 256, 0), (768, 128, channels)):
        quarter = 0
        for value in split_rows(*halves(load_rows(rows_ref, begin, width)), 4):
            for piece in split_rows(*halves(value), 2):
                if target + quarter * width < shared_ref.shape[1]:
                    store_parts(shared_ref, piece, 1, target + quarter * width)
                quarter += 1


def compact(rows, channels):
    row_count = rows.shape[0]
    return pl.pallas_call(
        functools.partial(compact_kernel, channels),
        out_shape=jax.ShapeDtypeStruct((row_count // 4, channels + REACH), jnp.bfloat16),
        in_specs=[pl.BlockSpec(memory_space=pltpu.VMEM)],
        out_specs=pl.BlockSpec(memory_space=pltpu.VMEM),
        compiler_params=params(16),
        cost_estimate=cost(0, 2 * 1024 * 1024),
        name="compact",
    )(rows)


def stack_kernel(rows_ref, out_ref, own_ref):
    row_count, channels = own_ref.shape
    block = 256
    for begin in (0, 256):
        for h, value in enumerate(split_rows(*halves(load_rows(rows_ref, begin, 256)), 4)):
            store_parts(own_ref, value, 2, h * 512 + begin)
    lane = lax.broadcasted_iota(jnp.int32, (16, 128), 1)
    flip = flip_matrix(block, block)
    for c in range(channels // block):
        left = dot(flip, own_ref[:, c * block : (c + 1) * block], 1, 1).astype(jnp.bfloat16)
        left = jnp.concatenate([left, turned(left, row_count // 2)], axis=0)
        products = band_products(left, own_ref, c * block, 2 * block, channels)
        for p in range(2):
            store_items(products[p * block : (p + 1) * block], c, p, out_ref, lane)


def stack(rows, channels, devices):
    return pl.pallas_call(
        stack_kernel,
        out_shape=jax.ShapeDtypeStruct((devices, 32, 128), jnp.bfloat16),
        in_specs=[pl.BlockSpec(memory_space=pltpu.VMEM)],
        out_specs=pl.BlockSpec(memory_space=pltpu.VMEM),
        scratch_shapes=[pltpu.VMEM((rows.shape[0] // 2, channels), jnp.bfloat16)],
        compiler_params=params(16),
        cost_estimate=cost(4 * 1024 * 512 * 512, 4 * 1024 * 1024),
        name="stack",
    )(rows)


def shared_kernel(info_ref, own_ref, other_ref, items_ref, out_hbm, *refs):
    rest_refs, (both_ref, item_ref, rest_ref, sems) = refs[:4], refs[4:]
    row_count, width = own_ref.shape
    channels = width - REACH
    block = 256
    copies = [pltpu.make_async_copy(items_ref, out_hbm.at[:, pl.ds(0, 32)], sems.at[0])]
    copies[0].start()
    lane = lax.broadcasted_iota(jnp.int32, (16, 128), 1)
    both_ref[:row_count] = own_ref[...]
    both_ref[row_count:] = other_ref[...]
    core = info_ref[0]

    def left_side(flip, begin):
        left = dot(flip, both_ref[:, begin : begin + flip.shape[0]], 1, 1).astype(jnp.bfloat16)
        return jnp.where(core == 0, left, turned(left, row_count // 2))

    flip = flip_matrix(block, block)
    for c in range(channels // block):
        products = band_products(left_side(flip, c * block), both_ref, c * block, 2 * block, channels)
        store_items(products, c, 0, item_ref, lane)
        where = pl.ds(c * 32, 32)
        copies.append(
            pltpu.make_async_copy(item_ref.at[where], out_hbm.at[where, pl.ds(32, 16)], sems.at[c + 1])
        )
        copies[-1].start()
    products = dot(left_side(flip_matrix(128, 128), channels), both_ref[:, channels:], 1, 0)
    for i in range(4):

        def store(j, value, i=i):
            rest_ref[jnp.bitwise_and(7 - i - info_ref[1], 3), j] = value

        skew_store(products[i * 32 : (i + 1) * 32], 257 + 32 * i, lane, store)
    for n, ref in enumerate(rest_refs):
        ref[...] = rest_ref[n]
    for copy in copies:
        copy.wait()


def stack_shared(info, own, other, items, devices):
    row_count, width = own.shape
    shapes = [(devices, 48, 128)] + [(4, 16, 128)] * 4
    return pl.pallas_call(
        shared_kernel,
        out_shape=[jax.ShapeDtypeStruct(shape, jnp.bfloat16) for shape in shapes],
        in_specs=[pl.BlockSpec(memory_space=pltpu.SMEM)] + [pl.BlockSpec(memory_space=pltpu.VMEM)] * 3,
        out_specs=[pl.BlockSpec(memory_space=pltpu.HBM)] + [pl.BlockSpec(memory_space=pltpu.VMEM)] * 4,
        scratch_shapes=[
            pltpu.VMEM((2 * row_count, width), jnp.bfloat16),
            pltpu.VMEM((devices, 16, 128), jnp.bfloat16),
            pltpu.VMEM((4, 4, 16, 128), jnp.bfloat16),
            pltpu.SemaphoreType.DMA((1 + (width - REACH) // 256,)),
        ],
        compiler_params=params(16),
        cost_estimate=cost(2 * 1024 * 512 * 512, 4 * 1024 * 1024),
        name="stack_shared",
    )(info, own, other, items)


def lag_kernel(parts, info_ref, table_ref, stacks_ref, rest_ref, out_hbm, wide_ref, last_ref, out_ref, sems):
    each = 16 // parts
    split = stacks_ref.shape[0]
    wide_ref[...] = stacks_ref[...].astype(jnp.float32)
    for k in range(4):
        source = jnp.bitwise_and(info_ref[1] + 4 - k, 3)
        for n in range(4):
            begin = pl.multiple_of((source * 4 + n) * 16, 16)
            last_ref[pl.ds(begin, 16), :] = rest_ref[n, k * 4 + info_ref[2]].astype(jnp.float32)
    swap = info_ref[0]
    copies = []
    for part in range(parts):
        sides = []
        for n in range(each):
            place = 15 - (part * each + n)
            side = [wide_ref[pl.ds(place, split // 16, stride=16), :], last_ref[pl.ds(place, 16, stride=16), :]]
            sides.append(jnp.concatenate(side, axis=0).astype(jnp.bfloat16))
        both = dot(jnp.concatenate(sides, axis=1), table_ref[...], 0, 0)
        lags = both[:, :LAGS] + both[:, LAGS:]
        for n in range(each):
            for h in range(2):
                r = n * 128 + h * 64
                out_ref[(h + swap) % 2, part * each + n] = lags[r : r + 64]
        where = (slice(None), pl.ds(part * each, each))
        copies.append(pltpu.make_async_copy(out_ref.at[where], out_hbm.at[where], sems.at[part]))
        copies[-1].start()
    for copy in copies:
        copy.wait()


def lag_transform(info, stacks, rest, devices):
    parts = 8
    table = jnp.asarray(lag_rows(devices))
    shape = (2, 16, 64, LAGS)
    out = pl.pallas_call(
        functools.partial(lag_kernel, parts),
        grid=(1,),
        in_specs=[
            pl.BlockSpec(memory_space=pltpu.SMEM),
            pl.BlockSpec(table.shape, lambda i: (0, 0)),
            pl.BlockSpec(stacks.shape, lambda i: (0, 0)),
            pl.BlockSpec(rest.shape, lambda i: (0, 0, 0, 0)),
        ],
        out_specs=pl.BlockSpec(memory_space=pltpu.HBM),
        out_shape=jax.ShapeDtypeStruct(shape, jnp.float32),
        scratch_shapes=[
            pltpu.VMEM(stacks.shape, jnp.float32),
            pltpu.VMEM((2 * GROUP * 16, 128), jnp.float32),
            pltpu.VMEM(shape, jnp.float32),
            pltpu.SemaphoreType.DMA((parts,)),
        ],
        compiler_params=params(24),
        cost_estimate=cost(4 * 2 * BINS * 2048 * 256, 4 * 1024 * 1024),
        name="lag_transform",
    )(info, table, stacks, rest)
    return out.reshape(32, 64, LAGS)


def per_device(chan_size, win_size, records):
    devices = chan_size * win_size
    axes = ("chan", "win")
    channels = records.shape[2]

    def exchange(array):
        return lax.all_to_all(array, axes, split_axis=0, concat_axis=0, tiled=True)

    chan, win = lax.axis_index("chan"), lax.axis_index("win")
    info = jnp.stack([win % 2, chan % 4, win]).astype(jnp.int32)
    rows = whiten(records, devices).reshape(devices, 8, LANES)
    rows, info = lax.optimization_barrier((rows, info))
    rows = exchange(rows).reshape(devices * 8, LANES)
    shared = compact(rows, channels)
    other = lax.ppermute(shared, "win", [(w, w ^ 1) for w in range(win_size)])
    items = stack(rows, channels, devices)
    stacks, *rest = stack_shared(info, shared, other, items, devices)
    for n in range(1, 4):
        rest[n] = lax.ppermute(rest[n], "chan", [(c, c // 4 * 4 + (c + n) % 4) for c in range(chan_size)])
    rest = lax.all_gather(jnp.concatenate(rest), "win")
    return lag_transform(info, exchange(stacks).reshape(devices * 48, 128), rest, devices)


def solution(mesh):
    in_specs = (P(("chan", "win"), None, None),)
    out_specs = P("chan", "win", None)
    body = functools.partial(per_device, mesh.shape["chan"], mesh.shape["win"])
    return jax.shard_map(body, mesh=mesh, in_specs=in_specs, out_specs=out_specs, check_vma=False)
```

```python
import functools
import math

import jax
import jax.numpy as jnp
import ml_dtypes
import numpy as np
from jax import lax
from jax.experimental import pallas as pl
from jax.experimental.pallas import tpu as pltpu
from jax.sharding import PartitionSpec as P

SAMPLES = 1000
BINS = 200
FIRST_BIN = 20
BAND = 256
LAGS = 256
WINDOWS = 256
GROUP = 8
REACH = 384
LANES = 896


def cos_sin(freqs, times):
    turns = freqs * times
    turns = turns - SAMPLES * jnp.floor(turns * (1.0 / SAMPLES) + 0.5)
    phase = turns * (2.0 * math.pi / SAMPLES)
    return jnp.cos(phase), jnp.sin(phase)


def dft_rows():
    def ramp(rows, axis):
        return lax.broadcasted_iota(jnp.int32, (rows, SAMPLES), axis).astype(jnp.float32)

    near_cos, near_sin = cos_sin(ramp(8, 0), ramp(8, 1))
    base_cos, base_sin = cos_sin(FIRST_BIN + 8.0 * ramp(32, 0), ramp(32, 1))
    real_rows, imag_rows = [], []
    for n in range(BINS // 8):
        far_cos, far_sin = base_cos[n : n + 1], base_sin[n : n + 1]
        real_rows.append(far_cos * near_cos - far_sin * near_sin)
        imag_rows.append(-far_sin * near_cos - far_cos * near_sin)
    return jnp.concatenate(real_rows + imag_rows, axis=0).astype(jnp.bfloat16)


def lag_rows(devices):
    owner = np.arange(devices)
    third = devices + owner // 2
    bins = np.stack([owner, owner, third], axis=1).reshape(-1)
    part = np.stack([0 * owner, 0 * owner + 1, owner % 2], axis=1).reshape(-1)
    last = np.arange(BINS - GROUP, BINS)
    bins = np.concatenate([bins, np.repeat(last, 2)])
    part = np.concatenate([part, np.tile([0, 1], GROUP)])
    shifts = np.arange(LAGS) - LAGS // 2
    phase = ((FIRST_BIN + bins)[:, None] * shifts[None, :] % SAMPLES) * (2.0 * math.pi / SAMPLES)
    table = np.where(part[:, None] == 0, np.cos(phase), -np.sin(phase)) / (WINDOWS * math.sqrt(BINS))
    high = table.astype(ml_dtypes.bfloat16)
    low = (table - high.astype(np.float64)).astype(ml_dtypes.bfloat16)
    return np.concatenate([high, low], axis=1)


def dot(left, right, left_dim, right_dim):
    dims = (((left_dim,), (right_dim,)), ((), ()))
    return lax.dot_general(left, right, dims, preferred_element_type=jnp.float32)


def params(mebibytes):
    return pltpu.CompilerParams(vmem_limit_bytes=mebibytes * 1024 * 1024)


def cost(flops, bytes_accessed):
    return pl.CostEstimate(flops=flops, bytes_accessed=bytes_accessed, transcendentals=0)


def whiten_kernel(devices, records_hbm, out_ref, records_ref, dft_ref, rows_ref, sems):
    windows, _, channels = records_ref.shape
    copies = []
    for w in range(windows):
        copies.append(pltpu.make_async_copy(records_hbm.at[w], records_ref.at[w], sems.at[w]))
        copies[-1].start()
    row = lax.broadcasted_iota(jnp.int32, (BINS, 2 * BINS), 0)
    column = lax.broadcasted_iota(jnp.int32, (BINS, 2 * BINS), 1)
    column = jnp.where(column < BINS, column, column - BINS)
    near = jnp.where(jnp.abs(row - column) <= 4, 1.0, 0.0).astype(jnp.bfloat16)
    place = lax.broadcasted_iota(jnp.int32, (BINS, 1), 0)
    count = jnp.minimum(place + 4, BINS - 1) - jnp.maximum(place - 4, 0) + 1
    weight = 1.0 / count.astype(jnp.float32)
    for r in (6, 7):
        rows_ref[6, pl.ds(r, devices, stride=8), :] = jnp.zeros((devices, 128), jnp.float32)
    dft_ref[...] = dft_rows()
    for w in range(windows):
        copies[w].wait()
        spectra = dot(dft_ref[...], records_ref[w], 1, 0)
        real_part = spectra[:BINS]
        imag_part = spectra[BINS:]
        power = real_part * real_part + imag_part * imag_part
        size = jnp.sqrt(power)
        high = size.astype(jnp.bfloat16).astype(jnp.float32)
        both = jnp.concatenate([high, size - high], axis=0).astype(jnp.bfloat16)
        smooth = dot(near, both, 1, 0) * weight
        level = jnp.sqrt(jnp.sum(power, axis=0, keepdims=True) * (1.0 / BINS) + 1e-06)
        scale = 1.0 / (smooth + 0.25 * level)
        for part, values in enumerate((real_part * scale, imag_part * scale)):
            for n in range(channels // 128):
                piece = values[:, n * 128 : (n + 1) * 128]
                place = pl.ds(n // 4 * 4 + part * 2 + w, devices, stride=8)
                rows_ref[n % 4, place, :] = piece[:devices]
                place = pl.ds(w * 8 + n // 2 * 2 + part, devices // 2, stride=16)
                rows_ref[4 + n % 2, place, :] = piece[devices : BINS - GROUP]
            last = values[BINS - GROUP :]
            last = jnp.concatenate([last, jnp.zeros((GROUP, REACH - 128), jnp.float32)], axis=1)
            for g in range(devices // (2 * GROUP)):
                for n in range(REACH // 128):
                    place = pl.ds(g * 16 * GROUP + w * 8 + n * 2 + part, GROUP, stride=16)
                    rows_ref[6, place, :] = last[:, (g + n) * 128 : (g + n + 1) * 128]
    for n in range(rows_ref.shape[0]):
        out_ref[:, n * 128 : (n + 1) * 128] = rows_ref[n].astype(jnp.bfloat16)


def whiten(records, devices):
    windows, samples, channels = records.shape
    rows = devices * 8
    return pl.pallas_call(
        functools.partial(whiten_kernel, devices),
        in_specs=[pl.BlockSpec(memory_space=pltpu.HBM)],
        out_specs=pl.BlockSpec(memory_space=pltpu.VMEM),
        out_shape=jax.ShapeDtypeStruct((rows, LANES), jnp.bfloat16),
        scratch_shapes=[
            pltpu.VMEM(records.shape, jnp.bfloat16),
            pltpu.VMEM((2 * BINS, samples), jnp.bfloat16),
            pltpu.VMEM((LANES // 128, rows, 128), jnp.float32),
            pltpu.SemaphoreType.DMA((windows,)),
        ],
        compiler_params=params(50),
        cost_estimate=cost(2 * windows * samples * channels * 2 * BINS, records.size * 2 + rows * channels * 2),
        name="whiten",
    )(records)


def split_rows(even, odd, gap):
    row = lax.broadcasted_iota(jnp.int32, (1, 8, even.shape[2]), 1)
    first = row // gap % 2 == 0
    return jnp.where(first, even, pltpu.roll(odd, gap, 1)), jnp.where(first, pltpu.roll(even, 8 - gap, 1), odd)


def flip_matrix(count, width):
    row = lax.broadcasted_iota(jnp.int32, (count, width), 0)
    column = lax.broadcasted_iota(jnp.int32, (count, width), 1)
    return jnp.where(row + column == count - 1, 1.0, 0.0).astype(jnp.bfloat16)


def turned(left, width):
    pieces = []
    for begin in range(0, left.shape[1], 2 * width):
        pieces += [left[:, begin + width : begin + 2 * width], -left[:, begin : begin + width]]
    return jnp.concatenate(pieces, axis=1)


def skew_store(part, shift, lane, store):
    second = pltpu.roll(part[:16], (shift + 64) % REACH, 1, stride=1, stride_axis=0)
    first = pltpu.roll(part[16:], (shift + 16) % REACH, 1, stride=1, stride_axis=0)
    for q in range(BAND // 128):
        now = slice(q * 128, (q + 1) * 128)
        then = slice((q + 1) * 128, (q + 2) * 128)
        store(2 * q, jnp.where(lane < 64, first[:, now], second[:, now]).astype(jnp.bfloat16))
        store(2 * q + 1, jnp.where(lane < 64, second[:, then], first[:, now]).astype(jnp.bfloat16))


def store_items(products, c, item, out_ref, lane):
    for i in range(8):
        begin = 128 * (1 - i // 4)
        part = products[i * 32 : (i + 1) * 32, begin : begin + REACH]

        def store(j, value, i=i):
            out_ref[(c * 8 + 7 - i) * 4 + j, item * 16 : (item + 1) * 16, :] = value

        skew_store(part, 257 + 32 * (i % 4), lane, store)


def band_products(left, right_ref, begin, width, channels):
    extent = min(width, channels - begin)
    products = dot(left, right_ref[:, begin : begin + extent], 1, 0)
    if extent < width:
        products = jnp.concatenate([products, jnp.zeros((left.shape[0], width - extent), jnp.float32)], axis=1)
    return products


def halves(value):
    value = value.reshape(value.shape[0] // 2, 2, 8, value.shape[2])
    return value[:, 0], value[:, 1]


def load_rows(rows_ref, begin, width):
    row_count = rows_ref.shape[0]
    return rows_ref[:, begin : begin + width].astype(jnp.float32).reshape(row_count // 8, 8, width)


def store_parts(ref, value, gap, begin):
    count, width = ref.shape[0] // 2, value.shape[2]
    for part, piece in enumerate(split_rows(*halves(value), gap)):
        where = slice(part * count, (part + 1) * count)
        ref[where, begin : begin + width] = piece.reshape(count, width).astype(jnp.bfloat16)


def compact_kernel(channels, rows_ref, shared_ref):
    for begin, width, target in ((512, 256, 0), (768, 128, channels)):
        quarter = 0
        for value in split_rows(*halves(load_rows(rows_ref, begin, width)), 4):
            for piece in split_rows(*halves(value), 2):
                if target + quarter * width < shared_ref.shape[1]:
                    store_parts(shared_ref, piece, 1, target + quarter * width)
                quarter += 1


def compact(rows, channels):
    row_count = rows.shape[0]
    return pl.pallas_call(
        functools.partial(compact_kernel, channels),
        out_shape=jax.ShapeDtypeStruct((row_count // 4, channels + REACH), jnp.bfloat16),
        in_specs=[pl.BlockSpec(memory_space=pltpu.VMEM)],
        out_specs=pl.BlockSpec(memory_space=pltpu.VMEM),
        compiler_params=params(16),
        cost_estimate=cost(0, 2 * 1024 * 1024),
        name="compact",
    )(rows)


def stack_kernel(rows_ref, out_ref, own_ref):
    row_count, channels = own_ref.shape
    block = 256
    for begin in (0, 256):
        for h, value in enumerate(split_rows(*halves(load_rows(rows_ref, begin, 256)), 4)):
            store_parts(own_ref, value, 2, h * 512 + begin)
    lane = lax.broadcasted_iota(jnp.int32, (16, 128), 1)
    flip = flip_matrix(block, block)
    for c in range(channels // block):
        left = dot(flip, own_ref[:, c * block : (c + 1) * block], 1, 1).astype(jnp.bfloat16)
        left = jnp.concatenate([left, turned(left, row_count // 2)], axis=0)
        products = band_products(left, own_ref, c * block, 2 * block, channels)
        for p in range(2):
            store_items(products[p * block : (p + 1) * block], c, p, out_ref, lane)


def stack(rows, channels, devices):
    return pl.pallas_call(
        stack_kernel,
        out_shape=jax.ShapeDtypeStruct((devices, 32, 128), jnp.bfloat16),
        in_specs=[pl.BlockSpec(memory_space=pltpu.VMEM)],
        out_specs=pl.BlockSpec(memory_space=pltpu.VMEM),
        scratch_shapes=[pltpu.VMEM((rows.shape[0] // 2, channels), jnp.bfloat16)],
        compiler_params=params(16),
        cost_estimate=cost(4 * 1024 * 512 * 512, 4 * 1024 * 1024),
        name="stack",
    )(rows)


def shared_kernel(info_ref, own_ref, other_ref, items_ref, out_hbm, *refs):
    rest_refs, (both_ref, item_ref, rest_ref, sems) = refs[:4], refs[4:]
    row_count, width = own_ref.shape
    channels = width - REACH
    block = 256
    copies = [pltpu.make_async_copy(items_ref, out_hbm.at[:, pl.ds(0, 32)], sems.at[0])]
    copies[0].start()
    lane = lax.broadcasted_iota(jnp.int32, (16, 128), 1)
    both_ref[:row_count] = own_ref[...]
    both_ref[row_count:] = other_ref[...]
    core = info_ref[0]

    def left_side(flip, begin):
        left = dot(flip, both_ref[:, begin : begin + flip.shape[0]], 1, 1).astype(jnp.bfloat16)
        return jnp.where(core == 0, left, turned(left, row_count // 2))

    flip = flip_matrix(block, block)
    for c in range(channels // block):
        products = band_products(left_side(flip, c * block), both_ref, c * block, 2 * block, channels)
        store_items(products, c, 0, item_ref, lane)
        where = pl.ds(c * 32, 32)
        copies.append(
            pltpu.make_async_copy(item_ref.at[where], out_hbm.at[where, pl.ds(32, 16)], sems.at[c + 1])
        )
        copies[-1].start()
    products = dot(left_side(flip_matrix(128, 128), channels), both_ref[:, channels:], 1, 0)
    for i in range(4):

        def store(j, value, i=i):
            rest_ref[jnp.bitwise_and(7 - i - info_ref[1], 3), j] = value

        skew_store(products[i * 32 : (i + 1) * 32], 257 + 32 * i, lane, store)
    for n, ref in enumerate(rest_refs):
        ref[...] = rest_ref[n]
    for copy in copies:
        copy.wait()


def stack_shared(info, own, other, items, devices):
    row_count, width = own.shape
    shapes = [(devices, 48, 128)] + [(4, 16, 128)] * 4
    return pl.pallas_call(
        shared_kernel,
        out_shape=[jax.ShapeDtypeStruct(shape, jnp.bfloat16) for shape in shapes],
        in_specs=[pl.BlockSpec(memory_space=pltpu.SMEM)] + [pl.BlockSpec(memory_space=pltpu.VMEM)] * 3,
        out_specs=[pl.BlockSpec(memory_space=pltpu.HBM)] + [pl.BlockSpec(memory_space=pltpu.VMEM)] * 4,
        scratch_shapes=[
            pltpu.VMEM((2 * row_count, width), jnp.bfloat16),
            pltpu.VMEM((devices, 16, 128), jnp.bfloat16),
            pltpu.VMEM((4, 4, 16, 128), jnp.bfloat16),
            pltpu.SemaphoreType.DMA((1 + (width - REACH) // 256,)),
        ],
        compiler_params=params(16),
        cost_estimate=cost(2 * 1024 * 512 * 512, 4 * 1024 * 1024),
        name="stack_shared",
    )(info, own, other, items)


def lag_kernel(parts, info_ref, table_ref, stacks_ref, rest_ref, out_hbm, wide_ref, last_ref, out_ref, sems):
    each = 16 // parts
    split = stacks_ref.shape[0]
    wide_ref[...] = stacks_ref[...].astype(jnp.float32)
    for k in range(4):
        source = jnp.bitwise_and(info_ref[1] + 4 - k, 3)
        for n in range(4):
            begin = pl.multiple_of((source * 4 + n) * 16, 16)
            last_ref[pl.ds(begin, 16), :] = rest_ref[n, k * 4 + info_ref[2]].astype(jnp.float32)
    swap = info_ref[0]
    copies = []
    for part in range(parts):
        sides = []
        for n in range(each):
            place = 15 - (part * each + n)
            side = [wide_ref[pl.ds(place, split // 16, stride=16), :], last_ref[pl.ds(place, 16, stride=16), :]]
            sides.append(jnp.concatenate(side, axis=0).astype(jnp.bfloat16))
        both = dot(jnp.concatenate(sides, axis=1), table_ref[...], 0, 0)
        lags = both[:, :LAGS] + both[:, LAGS:]
        for n in range(each):
            for h in range(2):
                r = n * 128 + h * 64
                out_ref[(h + swap) % 2, part * each + n] = lags[r : r + 64]
        where = (slice(None), pl.ds(part * each, each))
        copies.append(pltpu.make_async_copy(out_ref.at[where], out_hbm.at[where], sems.at[part]))
        copies[-1].start()
    for copy in copies:
        copy.wait()


def lag_transform(info, stacks, rest, devices):
    parts = 16
    table = jnp.asarray(lag_rows(devices))
    shape = (2, 16, 64, LAGS)
    out = pl.pallas_call(
        functools.partial(lag_kernel, parts),
        grid=(1,),
        in_specs=[
            pl.BlockSpec(memory_space=pltpu.SMEM),
            pl.BlockSpec(table.shape, lambda i: (0, 0)),
            pl.BlockSpec(stacks.shape, lambda i: (0, 0)),
            pl.BlockSpec(rest.shape, lambda i: (0, 0, 0, 0)),
        ],
        out_specs=pl.BlockSpec(memory_space=pltpu.HBM),
        out_shape=jax.ShapeDtypeStruct(shape, jnp.float32),
        scratch_shapes=[
            pltpu.VMEM(stacks.shape, jnp.float32),
            pltpu.VMEM((2 * GROUP * 16, 128), jnp.float32),
            pltpu.VMEM(shape, jnp.float32),
            pltpu.SemaphoreType.DMA((parts,)),
        ],
        compiler_params=params(24),
        cost_estimate=cost(4 * 2 * BINS * 2048 * 256, 4 * 1024 * 1024),
        name="lag_transform",
    )(info, table, stacks, rest)
    return out.reshape(32, 64, LAGS)


def per_device(chan_size, win_size, records):
    devices = chan_size * win_size
    axes = ("chan", "win")
    channels = records.shape[2]

    def exchange(array):
        return lax.all_to_all(array, axes, split_axis=0, concat_axis=0, tiled=True)

    chan, win = lax.axis_index("chan"), lax.axis_index("win")
    info = jnp.stack([win % 2, chan % 4, win]).astype(jnp.int32)
    rows = whiten(records, devices).reshape(devices, 8, LANES)
    rows, info = lax.optimization_barrier((rows, info))
    rows = exchange(rows).reshape(devices * 8, LANES)
    shared = compact(rows, channels)
    other = lax.ppermute(shared, "win", [(w, w ^ 1) for w in range(win_size)])
    items = stack(rows, channels, devices)
    stacks, *rest = stack_shared(info, shared, other, items, devices)
    for n in range(1, 4):
        rest[n] = lax.ppermute(rest[n], "chan", [(c, c // 4 * 4 + (c + n) % 4) for c in range(chan_size)])
    rest = lax.all_gather(jnp.concatenate(rest), "win")
    return lag_transform(info, exchange(stacks).reshape(devices * 48, 128), rest, devices)


def solution(mesh):
    in_specs = (P(("chan", "win"), None, None),)
    out_specs = P("chan", "win", None)
    body = functools.partial(per_device, mesh.shape["chan"], mesh.shape["win"])
    return jax.shard_map(body, mesh=mesh, in_specs=in_specs, out_specs=out_specs, check_vma=False)
```
